512 devices in a mesh: row: 32 (over z_lo, x, core), col: 16 (over y, z_hi).
Axes of the slice: x: 4, y: 4, z: 16 (z_hi: 4, z_lo: 4; z = z_hi * 4 + z_lo), core: 2. Of those that a mesh axis runs over, the one named last changes fastest.
Arguments:
- features: bfloat16 [131072, 128], P(('row', 'col')), may hold values from -6 to 6
- weight: bfloat16 [128, 128], replicated, may hold values from -0.5 to 0.5
- bias: float32 [128], replicated, may hold values from -3 to 3
- node_scale: float32 [131072], P(('row', 'col')), may hold values from 0.04 to 0.2
- cotangent: bfloat16 [131072, 128], P(('row', 'col')), may hold values from -6 to 6
- tile_row: int32 [32, 16, 8], P('row', 'col'), may hold values from 0 to 15
- tile_col: int32 [32, 16, 8], P('row', 'col'), may hold values from 0 to 31
- tile_count: int32 [32, 16], P('row', 'col'), may hold values from 1 to 8, as said below
- tile_values: bfloat16 [32, 16, 8, 256, 256], P('row', 'col'), may hold values from 0 to 1
Outputs:
- activated: bfloat16 [131072, 128], P(('row', 'col'))
- feature_grad: bfloat16 [131072, 128], P(('row', 'col'))
- weight_grad: float32 [128, 128], replicated
- bias_grad: float32 [128], replicated
The draws below stay inside these ranges and needn't reach their ends.
Inputs may be any that keep to these rules, and one draw needn't show every extreme that they name: `tile_count`: slots from this count on are ignored; in every draw some device has exactly 8 live slots.
All inputs are finite; a program needn't handle non-finite values.
Results may differ from the reference program's by a relative error of at most 0.015.
Values may be sent and summed in bfloat16 or wider, within the bound.
No kernel may reach another device: no remote copies, remote signals or barrier semaphores. Data moves between devices by JAX's collectives and lax.ppermute only.
A program may use at most 64 MiB of HBM per device.

```python
import math
import jax
import jax.numpy as jnp
from jax import lax

F = 128
BLOCK = 256
BPD = 1
TMAX = 8
NODES = 131072
ROWBLK = 16
COLBLK = 32
N_ROW = 32
N_COL = 16


def draw_tile_count(key, part):
    key = jax.random.fold_in(key, 7)
    first, second, third = jax.random.split(key, 3)
    counts = jax.random.randint(first, (N_ROW, N_COL), max(1, TMAX // 4), TMAX + 1)
    row_pick = jax.random.randint(second, (), 0, N_ROW)
    col_pick = jax.random.randint(third, (), 0, N_COL)
    return counts.at[row_pick, col_pick].set(TMAX).astype(jnp.int32)


def place_ends(entries, key, least, largest):
    index_at = [jax.random.randint(jax.random.fold_in(key, axis), (), 0, length) for axis, length in enumerate(entries.shape)]
    main_axis = entries.shape.index(max(entries.shape))
    beside = index_at[:main_axis] + [(index_at[main_axis] + 1) % entries.shape[main_axis]] + index_at[main_axis + 1:]
    return entries.at[tuple(index_at)].set(least).at[tuple(beside)].set(largest)


def steps_of(key, extent, pieces, least, high):
    def one(dim, shards_of):
        draws = jax.random.uniform(jax.random.fold_in(jax.random.fold_in(key, 6), dim), (shards_of,), jnp.float32, least / len(pieces), high / len(pieces))
        return jnp.repeat(jnp.exp(draws), extent[dim] // shards_of).reshape((-1,) + (1,) * (len(extent) - dim - 1))

    factor_of = one(*pieces[0])
    for cut in pieces[1:]:
        factor_of = factor_of * one(*cut)
    return factor_of


def centred(rng, extent, scale, bound, cuts=(), kind=jnp.bfloat16):
    values = scale * jax.random.normal(rng, extent, jnp.float32)
    if cuts:
        values = values * steps_of(rng, extent, cuts, -0.22, 0.18)
    return jnp.clip(values, -bound, bound).astype(kind)


def setup_inputs(seed: int = 0) -> dict:
    splits = jax.random.split(jax.random.key(seed), 10)
    features = centred(splits[0], (NODES, F), 1.0, 6.0, ((0, 512),))
    weight = centred(splits[1], (F, F), F ** -0.5, 0.5)
    bias = centred(splits[2], (F,), 0.5, 3.0, (), jnp.float32)
    node_scale = jnp.clip(jnp.exp(math.log(0.2) - 1.609438 * jax.random.uniform(splits[3], (NODES,), jnp.float32) ** steps_of(splits[3], (NODES,), ((0, 512),), -0.2, 0.2)), 0.04, 0.2)
    cotangent = centred(splits[4], (NODES, F), 1.0, 6.0, ((0, 512),))
    tile_row = place_ends(jax.random.randint(splits[5], (N_ROW, N_COL, TMAX), 0, ROWBLK), jax.random.fold_in(splits[5], 1), 0, ROWBLK - 1).astype(jnp.int32)
    tile_col = place_ends(jax.random.randint(splits[6], (N_ROW, N_COL, TMAX), 0, COLBLK), jax.random.fold_in(splits[6], 1), 0, COLBLK - 1).astype(jnp.int32)
    tile_count = draw_tile_count(jax.random.fold_in(splits[9], 71), 0)
    tile_values = jnp.clip(1.0 * jax.random.uniform(splits[8], (N_ROW, N_COL, TMAX, BLOCK, BLOCK), jnp.float32) ** steps_of(splits[8], (N_ROW, N_COL, TMAX, BLOCK, BLOCK), ((0, 32), (1, 16)), -0.2, 0.2), 0.0, 1.0).astype(jnp.bfloat16)
    return {"features": features, "weight": weight, "bias": bias, "node_scale": node_scale, "cotangent": cotangent, "tile_row": tile_row, "tile_col": tile_col, "tile_count": tile_count, "tile_values": tile_values}


def device_partials(x_five, tile_row, tile_col, tile_count, tile_values, dev):
    r = dev // N_COL
    c = dev % N_COL
    nbr = N_COL * BPD
    nbc = N_ROW * BPD
    x_rows = lax.dynamic_index_in_dim(x_five, r, 0, keepdims=False).reshape(nbr, BLOCK, F)
    x_cols = lax.dynamic_index_in_dim(x_five, c, 1, keepdims=False).reshape(nbc, BLOCK, F)
    rows_idx = tile_row[r, c]
    cols_idx = tile_col[r, c]
    count = tile_count[r, c]
    tiles = tile_values[r, c].astype(jnp.float32)
    slots = jnp.arange(TMAX, dtype=jnp.int32)
    glob_i = r * nbr + rows_idx
    glob_j = ((cols_idx // BPD) * N_COL + c) * BPD + cols_idx % BPD
    weights = jnp.where(slots < count, jnp.where(glob_i == glob_j, 0.5, 1.0), 0.0).astype(jnp.float32)
    row_hot = (jnp.arange(nbr, dtype=jnp.int32)[:, None] == rows_idx[None, :]).astype(jnp.float32) * weights[None, :]
    col_hot = (jnp.arange(nbc, dtype=jnp.int32)[:, None] == cols_idx[None, :]).astype(jnp.float32) * weights[None, :]
    row_terms = jnp.einsum("tab,tbf->taf", tiles, x_cols[cols_idx].astype(jnp.float32))
    col_terms = jnp.einsum("tab,taf->tbf", tiles, x_rows[rows_idx].astype(jnp.float32))
    row_part = jnp.einsum("it,taf->iaf", row_hot, row_terms).astype(jnp.bfloat16)
    col_part = jnp.einsum("jt,tbf->jbf", col_hot, col_terms).astype(jnp.bfloat16)
    return r, c, row_part, col_part


def aggregate(blocks, tile_row, tile_col, tile_count, tile_values):
    x_five = blocks.reshape(N_ROW, N_COL, BPD, BLOCK, F)

    def step(total, dev):
        r, c, row_part, col_part = device_partials(x_five, tile_row, tile_col, tile_count, tile_values, dev)
        row_slab = lax.dynamic_index_in_dim(total, r, 0, keepdims=False)
        row_slab = row_slab + row_part.astype(jnp.float32).reshape(N_COL, BPD, BLOCK, F)
        total = lax.dynamic_update_index_in_dim(total, row_slab, r, 0)
        col_slab = lax.dynamic_index_in_dim(total, c, 1, keepdims=False)
        col_slab = col_slab + col_part.astype(jnp.float32).reshape(N_ROW, BPD, BLOCK, F)
        total = lax.dynamic_update_index_in_dim(total, col_slab, c, 1)
        return total, None

    start = jnp.zeros((N_ROW, N_COL, BPD, BLOCK, F), jnp.float32)
    total, unused = lax.scan(step, start, jnp.arange(N_ROW * N_COL, dtype=jnp.int32))
    return total.reshape(NODES, F)


def reference(features, weight, bias, node_scale, cotangent, tile_row, tile_col, tile_count, tile_values):
    scale = node_scale[:, None]
    projected = (scale * jnp.dot(features, weight, preferred_element_type=jnp.float32)).astype(jnp.bfloat16)
    summed = aggregate(projected, tile_row, tile_col, tile_count, tile_values)
    preact = scale * (summed + projected.astype(jnp.float32)) + bias[None, :]
    activated = jax.nn.silu(preact).astype(jnp.bfloat16)
    sig = jax.nn.sigmoid(preact)
    delta = cotangent.astype(jnp.float32) * sig * (1.0 + preact * (1.0 - sig))
    scaled_delta = (scale * delta).astype(jnp.bfloat16)
    back = aggregate(scaled_delta, tile_row, tile_col, tile_count, tile_values)
    proj_grad = (scale * (back + scaled_delta.astype(jnp.float32))).astype(jnp.bfloat16)
    feature_grad = jnp.dot(proj_grad, weight.T, preferred_element_type=jnp.float32).astype(jnp.bfloat16)
    weight_grad = jnp.dot(features.T, proj_grad, preferred_element_type=jnp.float32)
    bias_grad = jnp.sum(delta, axis=0)
    return activated, feature_grad, weight_grad, bias_grad
```

```python
import jax
import jax.numpy as jnp
from jax import lax
from jax.experimental import pallas as pl
from jax.experimental.pallas import tpu as pltpu
from jax.sharding import PartitionSpec as P

BLOCK = 256
RING = 4
AXES = ("row", "col")


def rank(zl, x, core, y, zh):
    return ((zl * RING + x) * 2 + core) * RING * RING + y * RING + zh


def pairs(step):
    out = []
    for zl in range(RING):
        for x in range(RING):
            for core in range(2):
                for y in range(RING):
                    for zh in range(RING):
                        out.append((rank(zl, x, core, y, zh), rank(*step(zl, x, core, y, zh))))
    return out


def swap_cores(v):
    return lax.ppermute(v, AXES, pairs(lambda zl, x, core, y, zh: (zl, x, 1 - core, y, zh)))


def far_shift(v, k, row_core):
    def step(zl, x, core, y, zh):
        if core == row_core:
            return (zl + k) % RING, x, core, y, zh
        return zl, x, core, y, (zh + k) % RING

    return lax.ppermute(v, AXES, pairs(step))


def near_shift(v, k, row_core):
    def step(zl, x, core, y, zh):
        if core == row_core:
            return zl, (x + k) % RING, core, y, zh
        return zl, x, core, (y + k) % RING, zh

    return lax.ppermute(v, AXES, pairs(step))


def gather(both):
    far = jnp.concatenate([both] + [far_shift(both, k, 0) for k in range(1, RING)], axis=0)
    return jnp.concatenate([far] + [near_shift(far, k, 0) for k in range(1, RING)], axis=0)


def add_up(parts):
    total = parts[0].astype(jnp.float32)
    for part in parts[1:]:
        total = total + part.astype(jnp.float32)
    return total


def scatter_sum(parts):
    n = parts.shape[0] // RING
    near = [parts[k * n : (k + 1) * n] for k in range(RING)]
    near = add_up([near[0]] + [near_shift(near[k], k, 1) for k in range(1, RING)])
    near = near.astype(jnp.bfloat16)
    m = n // RING
    far = [near[k * m : (k + 1) * m] for k in range(RING)]
    return add_up([far[0]] + [far_shift(far[k], k, 1) for k in range(1, RING)])


def tile_kernel(src_ref, dst_ref, weight_ref, gathered_ref, own_ref, other_ref, out_ref, acc_ref):
    acc_ref[...] = jnp.zeros_like(acc_ref)
    slots = own_ref.shape[0]
    for half, tiles_ref in enumerate((own_ref, other_ref)):
        for t in range(slots):
            s = half * slots + t
            term = jnp.dot(
                tiles_ref[t], gathered_ref[src_ref[s]], preferred_element_type=jnp.float32
            )
            acc_ref[dst_ref[s]] += weight_ref[s] * term
    out_ref[...] = acc_ref[...].astype(out_ref.dtype)


def apply_tiles(src, dst, weights, gathered, own, other):
    smem = pl.BlockSpec(memory_space=pltpu.SMEM)
    vmem = pl.BlockSpec(memory_space=pltpu.VMEM)
    return pl.pallas_call(
        tile_kernel,
        out_shape=jax.ShapeDtypeStruct(gathered.shape, jnp.bfloat16),
        in_specs=[smem, smem, smem, vmem, vmem, vmem],
        out_specs=vmem,
        scratch_shapes=[pltpu.VMEM(gathered.shape, jnp.float32)],
        compiler_params=pltpu.CompilerParams(vmem_limit_bytes=32 * 1024 * 1024),
    )(src, dst, weights, gathered, own, other)


def shards(
    features, weight, bias, node_scale, cotangent, tile_row, tile_col, tile_count, tile_values
):
    row_pos = lax.axis_index("row")
    col_pos = lax.axis_index("col")
    core = row_pos % 2
    x = row_pos // 2 % RING
    zl = row_pos // (2 * RING)
    y = col_pos // RING
    zh = col_pos % RING
    n_col = lax.axis_size("col")
    first = core == 0

    rows_idx = tile_row[0, 0]
    cols_idx = tile_col[0, 0]
    tiles = tile_values[0, 0]
    slots = jnp.arange(rows_idx.shape[0], dtype=jnp.int32)
    same = row_pos * n_col + rows_idx == cols_idx * n_col + col_pos
    live = jnp.where(slots < tile_count[0, 0], jnp.where(same, 0.5, 1.0), 0.0)

    scale = node_scale[:, None]
    scaled = (scale * features.astype(jnp.float32)).astype(jnp.bfloat16)

    meta = jnp.stack([rows_idx.astype(jnp.float32), cols_idx.astype(jnp.float32), live])
    meta = jnp.pad(meta, ((0, 13), (0, 120))).astype(jnp.bfloat16)
    sent = swap_cores(jnp.concatenate([scaled, meta], axis=0))
    scaled_other = sent[:BLOCK]
    meta_other = sent[BLOCK : BLOCK + 3, :8]
    turned = jnp.swapaxes(tiles, 1, 2)
    own = jnp.where(first, tiles, turned)
    other = swap_cores(jnp.where(first, turned, tiles))

    rows_all = jnp.concatenate([rows_idx, meta_other[0].astype(jnp.int32)])
    cols_all = jnp.concatenate([cols_idx, meta_other[1].astype(jnp.int32)])
    weights = jnp.concatenate([live, meta_other[2].astype(jnp.float32)])
    foreign = jnp.concatenate([jnp.zeros_like(slots), jnp.ones_like(slots)])
    dx = cols_all // 2 % RING - x
    dzl = cols_all // (2 * RING) - zl
    dcore = (cols_all % 2 != core).astype(jnp.int32)
    dy = rows_all // RING - y
    dzh = rows_all % RING - zh
    from_row = (jnp.mod(-dx, RING) * RING + jnp.mod(-dzl, RING)) * 2 + dcore
    from_col = (jnp.mod(-dy, RING) * RING + jnp.mod(-dzh, RING)) * 2 + foreign
    to_row = (jnp.mod(dx, RING) * RING + jnp.mod(dzl, RING)) * 2 + dcore
    to_col = (jnp.mod(dy, RING) * RING + jnp.mod(dzh, RING)) * 2 + foreign
    src = jnp.where(first, from_row, from_col)
    dst = jnp.where(first, to_col, to_row)

    def aggregate(mine, theirs):
        gathered = gather(jnp.stack([mine, theirs]))
        sums = scatter_sum(apply_tiles(src, dst, weights, gathered, own, other))
        back = swap_cores(sums[1].astype(jnp.bfloat16))
        return sums[0] + back.astype(jnp.float32) + mine.astype(jnp.float32)

    spread = aggregate(scaled, scaled_other).astype(jnp.bfloat16)
    preact = scale * jnp.dot(spread, weight, preferred_element_type=jnp.float32) + bias[None, :]
    sig = jax.nn.sigmoid(preact)
    activated = jax.nn.silu(preact).astype(jnp.bfloat16)
    delta = cotangent.astype(jnp.float32) * sig * (1.0 + preact * (1.0 - sig))
    scaled_delta = (scale * delta).astype(jnp.bfloat16)

    local_weight = jnp.dot(spread.T, scaled_delta, preferred_element_type=jnp.float32)
    local_bias = jnp.sum(delta, axis=0, keepdims=True)
    grads = jnp.concatenate([local_weight, jnp.pad(local_bias, ((0, 7), (0, 0)))], axis=0)
    grads = lax.psum(lax.psum(grads, "row"), "col")

    proj_grad = scale * aggregate(scaled_delta, swap_cores(scaled_delta))
    feature_grad = jnp.dot(
        proj_grad.astype(jnp.bfloat16), weight.T, preferred_element_type=jnp.float32
    ).astype(jnp.bfloat16)
    n = weight.shape[0]
    return (activated, feature_grad, grads[:n], grads[n])


def solution(mesh):
    placed = (
        P(AXES, None),
        P(),
        P(),
        P(AXES),
        P(AXES, None),
        P("row", "col", None),
        P("row", "col", None),
        P("row", "col"),
        P("row", "col", None, None, None),
    )
    return jax.shard_map(
        shards,
        mesh=mesh,
        in_specs=placed,
        out_specs=(P(AXES, None), P(AXES, None), P(), P()),
        check_vma=False,
    )
```

```python
import functools
import jax
import jax.numpy as jnp
from jax import lax
from jax.experimental import pallas as pl
from jax.experimental.pallas import tpu as pltpu
from jax.sharding import PartitionSpec as P

BLOCK = 256
RING = 4
HALF = 64
LIFT = 80
AXES = ("row", "col")


def rank(zl, x, core, y, zh):
    return ((zl * RING + x) * 2 + core) * RING * RING + y * RING + zh


def pairs(step):
    out = []
    for zl in range(RING):
        for x in range(RING):
            for core in range(2):
                for y in range(RING):
                    for zh in range(RING):
                        out.append((rank(zl, x, core, y, zh), rank(*step(zl, x, core, y, zh))))
    return out


def swap_cores(v):
    return lax.ppermute(v, AXES, pairs(lambda zl, x, core, y, zh: (zl, x, 1 - core, y, zh)))


def far_shift(v, k, row_core):
    def step(zl, x, core, y, zh):
        if core == row_core:
            return (zl + k) % RING, x, core, y, zh
        return zl, x, core, y, (zh + k) % RING

    return lax.ppermute(v, AXES, pairs(step))


def near_shift(v, k, row_core):
    def step(zl, x, core, y, zh):
        if core == row_core:
            return zl, (x + k) % RING, core, y, zh
        return zl, x, core, (y + k) % RING, zh

    return lax.ppermute(v, AXES, pairs(step))


def call(kernel, outs, *operands, scalars=0, scratch=()):
    smem = pl.BlockSpec(memory_space=pltpu.SMEM)
    vmem = pl.BlockSpec(memory_space=pltpu.VMEM)
    return pl.pallas_call(
        kernel,
        out_shape=[jax.ShapeDtypeStruct(shape, dtype) for shape, dtype in outs],
        in_specs=[smem] * scalars + [vmem] * (len(operands) - scalars),
        out_specs=[vmem] * len(outs),
        scratch_shapes=list(scratch),
        compiler_params=pltpu.CompilerParams(vmem_limit_bytes=40 * 1024 * 1024),
    )(*operands)


def joined(ref, base):
    return ref[base : base + LIFT].astype(jnp.float32) + ref[
        base + LIFT : base + 2 * LIFT
    ].astype(jnp.float32)


def put_split(refs, base, value):
    high = value.astype(jnp.bfloat16)
    low = (value - high.astype(jnp.float32)).astype(jnp.bfloat16)
    for ref in refs:
        ref[base : base + LIFT] = high
        ref[base + LIFT : base + 2 * LIFT] = low


def put_lifted(refs, base_out, parts, base):
    own, after, across, before = [joined(ref, base) for ref in parts]
    put_split(refs, base_out, (own + across) + (after + before))


def join_kernel(lifted, *refs):
    parts, out_ref = refs[:RING], refs[RING]
    n = parts[0].shape[0] - lifted
    for k in range(RING):
        out_ref[k * n : (k + 1) * n] = parts[k][:n]
    if lifted:
        put_lifted([out_ref], RING * n, parts, n)


def tile_kernel(lifted, src_ref, dst_ref, weight_ref, own_ref, other_ref, *refs):
    parts, outs = refs[:RING], refs[RING : 2 * RING]
    gathered_ref, acc_ref = refs[2 * RING :]
    n = parts[0].shape[0] - lifted
    held = n // BLOCK
    for k in range(RING):
        gathered_ref[k * held : (k + 1) * held] = parts[k][:n].reshape(held, BLOCK, -1)
    acc_ref[...] = jnp.zeros_like(acc_ref)
    slots = own_ref.shape[0]
    for half, tiles_ref in enumerate((own_ref, other_ref)):
        for t in range(slots):
            s = half * slots + t
            term = jnp.dot(
                tiles_ref[t], gathered_ref[src_ref[s]], preferred_element_type=jnp.float32
            )
            acc_ref[dst_ref[s]] += weight_ref[s] * term
    for k in range(RING):
        sums = acc_ref[k * held : (k + 1) * held].astype(jnp.bfloat16)
        outs[k][:n] = sums.reshape(n, sums.shape[-1])
    if lifted:
        put_lifted(outs, n, parts, n)


def sum_kernel(lifted, *refs):
    parts, outs = refs[:RING], refs[RING:]
    n = parts[0].shape[0] - lifted
    m = n // RING
    for k in range(RING):
        total = parts[0][k * m : (k + 1) * m].astype(jnp.float32)
        for part in parts[1:]:
            total = total + part[k * m : (k + 1) * m].astype(jnp.float32)
        outs[k][:m] = total.astype(jnp.bfloat16)
    if lifted:
        put_lifted(outs, m, parts, n)


def last_kernel(lifted, *refs):
    parts, (own_ref, out_ref) = refs[:RING], refs[RING:]
    for k in range(2):
        rows = slice(k * BLOCK, (k + 1) * BLOCK)
        total = parts[0][rows].astype(jnp.float32)
        for part in parts[1:]:
            total = total + part[rows].astype(jnp.float32)
        if k == 0:
            own_ref[...] = total
        else:
            out_ref[:BLOCK] = total.astype(jnp.bfloat16)
    if lifted:
        put_lifted([out_ref], BLOCK, parts, 2 * BLOCK)


def middle_kernel(
    core_ref, own_ref, back_ref, scaled_ref, scale_ref, weight_ref, bias_ref, cotangent_ref,
    activated_ref, sent_ref, kept_ref,
):
    scale = scale_ref[...]
    total = own_ref[...] + back_ref[...].astype(jnp.float32) + scaled_ref[...].astype(jnp.float32)
    spread = total.astype(jnp.bfloat16)
    hidden = jnp.dot(spread, weight_ref[...], preferred_element_type=jnp.float32)
    preact = scale * hidden + bias_ref[...]
    sig = jax.nn.sigmoid(preact)
    activated_ref[...] = (preact * sig).astype(jnp.bfloat16)
    delta = cotangent_ref[...].astype(jnp.float32) * sig * (1.0 + preact * (1.0 - sig))
    scaled_delta = (scale * delta).astype(jnp.bfloat16)
    sent_ref[:BLOCK] = scaled_delta
    grads = lax.dot_general(
        spread, scaled_delta, (((0,), (0,)), ((), ())), preferred_element_type=jnp.float32
    )
    pad = LIFT - HALF
    bias_grad = jnp.sum(delta, axis=0, keepdims=True)
    row = lax.broadcasted_iota(jnp.int32, (pad, grads.shape[1]), 0)
    top = jnp.concatenate([grads[:HALF], jnp.where(row == 0, bias_grad, 0.0)], axis=0)
    bottom = jnp.concatenate([grads[HALF:], jnp.zeros((pad, grads.shape[1]), jnp.float32)], axis=0)
    first = core_ref[0] == 0
    put_split([kept_ref], 0, jnp.where(first, top, bottom))
    put_split([sent_ref], BLOCK, jnp.where(first, bottom, top))


def start_kernel(own_ref, kept_ref, other_ref, out_ref):
    out_ref[:BLOCK] = own_ref[:BLOCK]
    out_ref[BLOCK : 2 * BLOCK] = other_ref[:BLOCK]
    put_split([out_ref], 2 * BLOCK, joined(kept_ref, 0) + joined(other_ref, BLOCK))


def end_kernel(
    core_ref, own_ref, sent_ref, back_ref, mine_ref, scale_ref, weight_ref,
    feature_grad_ref, weight_grad_ref, bias_grad_ref,
):
    total = own_ref[...] + back_ref[:BLOCK].astype(jnp.float32)
    total = total + mine_ref[:BLOCK].astype(jnp.float32)
    proj_grad = (scale_ref[...] * total).astype(jnp.bfloat16)
    feature_grad_ref[...] = lax.dot_general(
        proj_grad, weight_ref[...], (((1,), (1,)), ((), ())), preferred_element_type=jnp.float32
    ).astype(jnp.bfloat16)
    first = core_ref[0] == 0
    here, there = joined(sent_ref, BLOCK), joined(back_ref, BLOCK)
    top = jnp.where(first, here, there)
    bottom = jnp.where(first, there, here)
    weight_grad_ref[:HALF] = top[:HALF]
    weight_grad_ref[HALF:] = bottom[:HALF]
    bias_grad_ref[...] = top[HALF : HALF + 1]


def shards(
    features, weight, bias, node_scale, cotangent, tile_row, tile_col, tile_count, tile_values
):
    row_pos = lax.axis_index("row")
    col_pos = lax.axis_index("col")
    core = row_pos % 2
    x = row_pos // 2 % RING
    zl = row_pos // (2 * RING)
    y = col_pos // RING
    zh = col_pos % RING
    n_col = lax.axis_size("col")
    first = core == 0
    width = features.shape[1]

    rows_idx = tile_row[0, 0]
    cols_idx = tile_col[0, 0]
    tiles = tile_values[0, 0]
    slots = jnp.arange(rows_idx.shape[0], dtype=jnp.int32)
    same = row_pos * n_col + rows_idx == cols_idx * n_col + col_pos
    live = jnp.where(slots < tile_count[0, 0], jnp.where(same, 0.5, 1.0), 0.0)

    scale = node_scale[:, None]
    scaled = (scale * features.astype(jnp.float32)).astype(jnp.bfloat16)

    meta = jnp.stack([rows_idx.astype(jnp.float32), cols_idx.astype(jnp.float32), live])
    meta = jnp.pad(meta, ((0, 13), (0, 120))).astype(jnp.bfloat16)
    arrived = swap_cores(jnp.concatenate([scaled, meta], axis=0))
    meta_other = arrived[BLOCK : BLOCK + 3, :8]
    turned = jnp.swapaxes(tiles, 1, 2)
    own = jnp.where(first, tiles, turned)
    other = swap_cores(jnp.where(first, turned, tiles))

    rows_all = jnp.concatenate([rows_idx, meta_other[0].astype(jnp.int32)])
    cols_all = jnp.concatenate([cols_idx, meta_other[1].astype(jnp.int32)])
    weights = jnp.concatenate([live, meta_other[2].astype(jnp.float32)])
    foreign = jnp.concatenate([jnp.zeros_like(slots), jnp.ones_like(slots)])
    dx = cols_all // 2 % RING - x
    dzl = cols_all // (2 * RING) - zl
    dcore = (cols_all % 2 != core).astype(jnp.int32)
    dy = rows_all // RING - y
    dzh = rows_all % RING - zh
    from_row = (jnp.mod(-dx, RING) * RING + jnp.mod(-dzl, RING)) * 2 + dcore
    from_col = (jnp.mod(-dy, RING) * RING + jnp.mod(-dzh, RING)) * 2 + foreign
    to_row = (jnp.mod(dx, RING) * RING + jnp.mod(dzl, RING)) * 2 + dcore
    to_col = (jnp.mod(dy, RING) * RING + jnp.mod(dzh, RING)) * 2 + foreign
    src = jnp.where(first, from_row, from_col)
    dst = jnp.where(first, to_col, to_row)

    def aggregate(both, lifted):
        bf16 = jnp.bfloat16
        n, m = 2 * RING * BLOCK, 2 * BLOCK
        far = [both] + [far_shift(both, k, 0) for k in range(1, RING)]
        (held,) = call(
            functools.partial(join_kernel, lifted), [((n + lifted, width), bf16)], *far
        )
        near = [held] + [near_shift(held, k, 0) for k in range(1, RING)]
        slabs = (2 * RING * RING, BLOCK, width)
        sums = call(
            functools.partial(tile_kernel, lifted),
            [((n + lifted, width), bf16)] * RING,
            src, dst, weights, own, other, *near,
            scalars=3,
            scratch=[pltpu.VMEM(slabs, bf16), pltpu.VMEM(slabs, jnp.float32)],
        )
        near = [sums[0]] + [near_shift(sums[k], k, 1) for k in range(1, RING)]
        sums = call(
            functools.partial(sum_kernel, lifted), [((m + lifted, width), bf16)] * RING, *near
        )
        far = [sums[0]] + [far_shift(sums[k], k, 1) for k in range(1, RING)]
        mine, theirs = call(
            functools.partial(last_kernel, lifted),
            [((BLOCK, width), jnp.float32), ((BLOCK + lifted, width), bf16)],
            *far,
        )
        return mine, theirs, swap_cores(theirs)

    lifted = 2 * LIFT
    core_no = core.reshape(1)
    mine, _, back = aggregate(jnp.concatenate([scaled, arrived[:BLOCK]], axis=0), 0)
    activated, sent, kept = call(
        middle_kernel,
        [
            ((BLOCK, width), jnp.bfloat16),
            ((BLOCK + lifted, width), jnp.bfloat16),
            ((lifted, width), jnp.bfloat16),
        ],
        core_no, mine, back, scaled, scale, weight, bias[None, :], cotangent,
        scalars=1,
    )
    (both,) = call(
        start_kernel,
        [((2 * BLOCK + lifted, width), jnp.bfloat16)],
        sent, kept, swap_cores(sent),
    )
    mine, theirs, back = aggregate(both, lifted)
    feature_grad, weight_grad, bias_grad = call(
        end_kernel,
        [
            ((BLOCK, width), jnp.bfloat16),
            (weight.shape, jnp.float32),
            ((1, width), jnp.float32),
        ],
        core_no, mine, theirs, back, sent, scale, weight,
        scalars=1,
    )
    return activated, feature_grad, weight_grad, bias_grad[0]


def solution(mesh):
    placed = (
        P(AXES, None),
        P(),
        P(),
        P(AXES),
        P(AXES, None),
        P("row", "col", None),
        P("row", "col", None),
        P("row", "col"),
        P("row", "col", None, None, None),
    )
    return jax.shard_map(
        shards,
        mesh=mesh,
        in_specs=placed,
        out_specs=(P(AXES, None), P(AXES, None), P(), P()),
        check_vma=False,
    )
```

```python
import functools
import jax
import jax.numpy as jnp
from jax import lax
from jax.experimental import pallas as pl
from jax.experimental.pallas import tpu as pltpu
from jax.sharding import PartitionSpec as P

BLOCK = 256
RING = 4
HALF = 64
LIFT = 80
AXES = ("row", "col")


def rank(zl, x, core, y, zh):
    return ((zl * RING + x) * 2 + core) * RING * RING + y * RING + zh


def pairs(step):
    out = []
    for zl in range(RING):
        for x in range(RING):
            for core in range(2):
                for y in range(RING):
                    for zh in range(RING):
                        out.append((rank(zl, x, core, y, zh), rank(*step(zl, x, core, y, zh))))
    return out


def swap_cores(v):
    return lax.ppermute(v, AXES, pairs(lambda zl, x, core, y, zh: (zl, x, 1 - core, y, zh)))


def far_shift(v, k, row_core):
    def step(zl, x, core, y, zh):
        if core == row_core:
            return (zl + k) % RING, x, core, y, zh
        return zl, x, core, y, (zh + k) % RING

    return lax.ppermute(v, AXES, pairs(step))


def near_shift(v, k, row_core):
    def step(zl, x, core, y, zh):
        if core == row_core:
            return zl, (x + k) % RING, core, y, zh
        return zl, x, core, (y + k) % RING, zh

    return lax.ppermute(v, AXES, pairs(step))


def call(kernel, outs, *operands, scalars=0, scratch=()):
    smem = pl.BlockSpec(memory_space=pltpu.SMEM)
    vmem = pl.BlockSpec(memory_space=pltpu.VMEM)
    return pl.pallas_call(
        kernel,
        out_shape=[jax.ShapeDtypeStruct(shape, dtype) for shape, dtype in outs],
        in_specs=[smem] * scalars + [vmem] * (len(operands) - scalars),
        out_specs=[vmem] * len(outs),
        scratch_shapes=list(scratch),
        compiler_params=pltpu.CompilerParams(vmem_limit_bytes=40 * 1024 * 1024),
    )(*operands)


def joined(ref, base, pieces):
    value = ref[base : base + LIFT].astype(jnp.float32)
    if pieces == 2:
        value = value + ref[base + LIFT : base + 2 * LIFT].astype(jnp.float32)
    return value


def put_split(refs, base, pieces, value):
    high = value.astype(jnp.bfloat16)
    low = (value - high.astype(jnp.float32)).astype(jnp.bfloat16)
    for ref in refs:
        ref[base : base + LIFT] = high
        if pieces == 2:
            ref[base + LIFT : base + 2 * LIFT] = low


def put_lifted(refs, base_out, pieces_out, parts, base, pieces):
    own, after, across, before = [joined(ref, base, pieces) for ref in parts]
    put_split(refs, base_out, pieces_out, (own + across) + (after + before))


def join_kernel(lift, *refs):
    parts, out_ref = refs[:RING], refs[RING]
    n = 2 * BLOCK
    for k in range(RING):
        out_ref[k * n : (k + 1) * n] = parts[k][:n]
    if lift:
        put_lifted([out_ref], RING * n, 2, parts, n, 1)


def tile_kernel(lift, src_ref, dst_ref, weight_ref, own_ref, other_ref, *refs):
    parts, outs = refs[:RING], refs[RING : 2 * RING]
    gathered_ref, acc_ref = refs[2 * RING :]
    held = 2 * RING
    n = held * BLOCK
    for k in range(RING):
        gathered_ref[k * held : (k + 1) * held] = parts[k][:n].reshape(held, BLOCK, -1)
    acc_ref[...] = jnp.zeros_like(acc_ref)
    slots = own_ref.shape[0]
    for half, tiles_ref in enumerate((own_ref, other_ref)):
        for t in range(slots):
            s = half * slots + t
            term = jnp.dot(
                tiles_ref[t], gathered_ref[src_ref[s]], preferred_element_type=jnp.float32
            )
            acc_ref[dst_ref[s]] += weight_ref[s] * term
    for k in range(RING):
        sums = acc_ref[k * held : (k + 1) * held].astype(jnp.bfloat16)
        outs[k][:n] = sums.reshape(n, sums.shape[-1])
    if lift:
        put_lifted(outs, n, 2, parts, n, 2)


def sum_kernel(lift, *refs):
    parts, outs = refs[:RING], refs[RING:]
    m = 2 * BLOCK
    for k in range(RING):
        total = parts[0][k * m : (k + 1) * m].astype(jnp.float32)
        for part in parts[1:]:
            total = total + part[k * m : (k + 1) * m].astype(jnp.float32)
        outs[k][:m] = total.astype(jnp.bfloat16)
    if lift:
        put_lifted(outs, m, 1, parts, RING * m, 2)


def relay_kernel(lift, mine_ref, passing_ref, out_ref):
    m = 2 * BLOCK
    total = mine_ref[:m].astype(jnp.float32) + passing_ref[:m].astype(jnp.float32)
    out_ref[:m] = total.astype(jnp.bfloat16)
    if lift:
        out_ref[m:] = passing_ref[m:]


def last_kernel(lift, own_ref, after_ref, across_ref, before_ref, sums_ref, out_ref):
    m = 2 * BLOCK
    total = own_ref[:m].astype(jnp.float32)
    for part in (across_ref, before_ref):
        total = total + part[:m].astype(jnp.float32)
    sums_ref[...] = total
    if lift:
        out_ref[:BLOCK] = total[BLOCK:].astype(jnp.bfloat16)
        parts = (own_ref, after_ref, across_ref, before_ref)
        put_lifted([out_ref], BLOCK, 2, parts, m, 1)
    else:
        out_ref[...] = total.astype(jnp.bfloat16)


def middle_kernel(
    core_ref, sums_ref, back_ref, both_ref, scale_ref, other_ref, weight_ref, bias_ref,
    cotangent_ref, activated_ref, out_ref,
):
    packed = other_ref[BLOCK : 2 * BLOCK, :3].astype(jnp.float32)
    scales = (scale_ref[...], packed[:, 0:1] + packed[:, 1:2] + packed[:, 2:3])
    cotangents = (cotangent_ref[...], other_ref[:BLOCK])
    grads = bias_grad = None
    for c in range(2):
        rows = slice(c * BLOCK, (c + 1) * BLOCK)
        back = back_ref[(1 - c) * BLOCK : (2 - c) * BLOCK].astype(jnp.float32)
        total = sums_ref[rows] + back + both_ref[rows].astype(jnp.float32)
        spread = total.astype(jnp.bfloat16)
        hidden = jnp.dot(spread, weight_ref[...], preferred_element_type=jnp.float32)
        preact = scales[c] * hidden + bias_ref[...]
        sig = jax.nn.sigmoid(preact)
        if c == 0:
            activated_ref[...] = (preact * sig).astype(jnp.bfloat16)
        delta = cotangents[c].astype(jnp.float32) * sig * (1.0 + preact * (1.0 - sig))
        scaled_delta = (scales[c] * delta).astype(jnp.bfloat16)
        out_ref[rows] = scaled_delta
        product = lax.dot_general(
            spread, scaled_delta, (((0,), (0,)), ((), ())), preferred_element_type=jnp.float32
        )
        column = jnp.sum(delta, axis=0, keepdims=True)
        grads = product if c == 0 else grads + product
        bias_grad = column if c == 0 else bias_grad + column
    pad = LIFT - HALF
    row = lax.broadcasted_iota(jnp.int32, (pad, grads.shape[1]), 0)
    top = jnp.concatenate([grads[:HALF], jnp.where(row == 0, bias_grad, 0.0)], axis=0)
    bottom = jnp.concatenate([grads[HALF:], jnp.zeros((pad, grads.shape[1]), jnp.float32)], axis=0)
    put_split([out_ref], 2 * BLOCK, 1, jnp.where(core_ref[0] == 0, top, bottom))


def end_kernel(
    core_ref, sums_ref, sent_ref, back_ref, both_ref, scale_ref, weight_ref,
    feature_grad_ref, weight_grad_ref, bias_grad_ref,
):
    total = sums_ref[:BLOCK] + back_ref[:BLOCK].astype(jnp.float32)
    total = total + both_ref[:BLOCK].astype(jnp.float32)
    proj_grad = (scale_ref[...] * total).astype(jnp.bfloat16)
    feature_grad_ref[...] = lax.dot_general(
        proj_grad, weight_ref[...], (((1,), (1,)), ((), ())), preferred_element_type=jnp.float32
    ).astype(jnp.bfloat16)
    first = core_ref[0] == 0
    here, there = joined(sent_ref, BLOCK, 2), joined(back_ref, BLOCK, 2)
    top = jnp.where(first, here, there)
    bottom = jnp.where(first, there, here)
    weight_grad_ref[:HALF] = top[:HALF]
    weight_grad_ref[HALF:] = bottom[:HALF]
    bias_grad_ref[...] = top[HALF : HALF + 1]


def shards(
    features, weight, bias, node_scale, cotangent, tile_row, tile_col, tile_count, tile_values
):
    row_pos = lax.axis_index("row")
    col_pos = lax.axis_index("col")
    core = row_pos % 2
    x = row_pos // 2 % RING
    zl = row_pos // (2 * RING)
    y = col_pos // RING
    zh = col_pos % RING
    n_col = lax.axis_size("col")
    first = core == 0
    width = features.shape[1]

    rows_idx = tile_row[0, 0]
    cols_idx = tile_col[0, 0]
    tiles = tile_values[0, 0]
    slots = jnp.arange(rows_idx.shape[0], dtype=jnp.int32)
    same = row_pos * n_col + rows_idx == cols_idx * n_col + col_pos
    live = jnp.where(slots < tile_count[0, 0], jnp.where(same, 0.5, 1.0), 0.0)

    scale = node_scale[:, None]
    scaled = (scale * features.astype(jnp.float32)).astype(jnp.bfloat16)

    meta = jnp.stack([rows_idx.astype(jnp.float32), cols_idx.astype(jnp.float32), live])
    meta = jnp.pad(meta, ((0, 13), (0, 120))).astype(jnp.bfloat16)
    arrived = swap_cores(jnp.concatenate([scaled, meta], axis=0))
    meta_other = arrived[BLOCK : BLOCK + 3, :8]
    rows_all = jnp.concatenate([rows_idx, meta_other[0].astype(jnp.int32)])
    cols_all = jnp.concatenate([cols_idx, meta_other[1].astype(jnp.int32)])
    weights = jnp.concatenate([live, meta_other[2].astype(jnp.float32)])
    foreign = jnp.concatenate([jnp.zeros_like(slots), jnp.ones_like(slots)])
    dx = cols_all // 2 % RING - x
    dzl = cols_all // (2 * RING) - zl
    dcore = (cols_all % 2 != core).astype(jnp.int32)
    dy = rows_all // RING - y
    dzh = rows_all % RING - zh
    from_row = (jnp.mod(-dx, RING) * RING + jnp.mod(-dzl, RING)) * 2 + dcore
    from_col = (jnp.mod(-dy, RING) * RING + jnp.mod(-dzh, RING)) * 2 + foreign
    to_row = (jnp.mod(dx, RING) * RING + jnp.mod(dzl, RING)) * 2 + dcore
    to_col = (jnp.mod(dy, RING) * RING + jnp.mod(dzh, RING)) * 2 + foreign
    src = jnp.where(first, from_row, from_col)
    dst = jnp.where(first, to_col, to_row)

    def gather_far(both, lift):
        after = far_shift(both, 1, 0)
        before = far_shift(both, -1, 0)
        across = far_shift(after, 1, 0)
        rows = 2 * RING * BLOCK + (2 * LIFT if lift else 0)
        (held,) = call(
            functools.partial(join_kernel, lift),
            [((rows, width), jnp.bfloat16)],
            both, after, across, before,
        )
        return held, after

    def spread_sum(held, own, other, lift):
        bf16 = jnp.bfloat16
        m = 2 * BLOCK + (LIFT if lift else 0)
        near = [held] + [near_shift(held, k, 0) for k in range(1, RING)]
        slabs = (2 * RING * RING, BLOCK, width)
        sums = call(
            functools.partial(tile_kernel, lift),
            [(held.shape, bf16)] * RING,
            src, dst, weights, own, other, *near,
            scalars=3,
            scratch=[pltpu.VMEM(slabs, bf16), pltpu.VMEM(slabs, jnp.float32)],
        )
        near = [sums[0]] + [near_shift(sums[k], k, 1) for k in range(1, RING)]
        sums = call(functools.partial(sum_kernel, lift), [((m, width), bf16)] * RING, *near)
        after = far_shift(sums[2], 1, 1)
        before = far_shift(sums[3], -1, 1)
        (passed,) = call(
            functools.partial(relay_kernel, lift), [((m, width), bf16)], sums[1], after
        )
        across = far_shift(passed, 1, 1)
        rows = BLOCK + 2 * LIFT if lift else 2 * BLOCK
        both_sums, sent = call(
            functools.partial(last_kernel, lift),
            [((2 * BLOCK, width), jnp.float32), ((rows, width), bf16)],
            sums[0], after, across, before,
        )
        return both_sums, sent, swap_cores(sent)

    core_no = core.reshape(1)
    both = jnp.concatenate([scaled, arrived[:BLOCK]], axis=0)
    held, after = gather_far(both, False)

    tiles, _ = lax.optimization_barrier((tiles, after))
    cotangent, parts, held = lax.optimization_barrier((cotangent, scale, held))
    turned = jnp.swapaxes(tiles, 1, 2)
    own = jnp.where(first, tiles, turned)
    other = swap_cores(jnp.where(first, turned, tiles))
    packed = []
    for _ in range(3):
        piece = lax.reduce_precision(parts, exponent_bits=8, mantissa_bits=7)
        packed.append(piece)
        parts = parts - piece
    packed = jnp.pad(jnp.concatenate(packed, axis=1), ((0, 0), (0, width - 3)))
    facts = swap_cores(jnp.concatenate([cotangent, packed.astype(jnp.bfloat16)], axis=0))

    sums, _, back = spread_sum(held, own, other, False)
    activated, both = call(
        middle_kernel,
        [((BLOCK, width), jnp.bfloat16), ((2 * BLOCK + LIFT, width), jnp.bfloat16)],
        core_no, sums, back, both, scale, facts, weight, bias[None, :], cotangent,
        scalars=1,
    )
    held, _ = gather_far(both, True)
    sums, sent, back = spread_sum(held, own, other, True)
    feature_grad, weight_grad, bias_grad = call(
        end_kernel,
        [
            ((BLOCK, width), jnp.bfloat16),
            (weight.shape, jnp.float32),
            ((1, width), jnp.float32),
        ],
        core_no, sums, sent, back, both, scale, weight,
        scalars=1,
    )
    return activated, feature_grad, weight_grad, bias_grad[0]


def solution(mesh):
    placed = (
        P(AXES, None),
        P(),
        P(),
        P(AXES),
        P(AXES, None),
        P("row", "col", None),
        P("row", "col", None),
        P("row", "col"),
        P("row", "col", None, None, None),
    )
    return jax.shard_map(
        shards,
        mesh=mesh,
        in_specs=placed,
        out_specs=(P(AXES, None), P(AXES, None), P(), P()),
        check_vma=False,
    )
```

```python
import functools
import jax
import jax.numpy as jnp
from jax import lax
from jax.experimental import pallas as pl
from jax.experimental.pallas import tpu as pltpu
from jax.sharding import PartitionSpec as P

BLOCK = 256
RING = 4
HALF = 64
LIFT = 80
AXES = ("row", "col")


def rank(zl, x, core, y, zh):
    return ((zl * RING + x) * 2 + core) * RING * RING + y * RING + zh


def pairs(step):
    out = []
    for zl in range(RING):
        for x in range(RING):
            for core in range(2):
                for y in range(RING):
                    for zh in range(RING):
                        out.append((rank(zl, x, core, y, zh), rank(*step(zl, x, core, y, zh))))
    return out


def swap_cores(v):
    return lax.ppermute(v, AXES, pairs(lambda zl, x, core, y, zh: (zl, x, 1 - core, y, zh)))


def groups(row_core, near):
    out = []
    for core in range(2):
        for free in range(RING**3):
            i, j, k = free // RING**2, free // RING % RING, free % RING
            if core == row_core:
                four = [rank(i, m, core, j, k) if near else rank(m, i, core, j, k) for m in range(RING)]
            else:
                four = [rank(i, j, core, m, k) if near else rank(i, j, core, k, m) for m in range(RING)]
            out.append(four)
    return out


def exchange(v, row_core, near):
    return lax.all_to_all(
        v, AXES, split_axis=0, concat_axis=0, tiled=True, axis_index_groups=groups(row_core, near)
    )


def call(kernel, outs, *operands, scalars=0, scratch=()):
    smem = pl.BlockSpec(memory_space=pltpu.SMEM)
    vmem = pl.BlockSpec(memory_space=pltpu.VMEM)
    return pl.pallas_call(
        kernel,
        out_shape=[jax.ShapeDtypeStruct(shape, dtype) for shape, dtype in outs],
        in_specs=[smem] * scalars + [vmem] * (len(operands) - scalars),
        out_specs=[vmem] * len(outs),
        scratch_shapes=list(scratch),
        compiler_params=pltpu.CompilerParams(vmem_limit_bytes=40 * 1024 * 1024),
    )(*operands)


def joined(ref, base, pieces):
    value = ref[base : base + LIFT].astype(jnp.float32)
    if pieces == 2:
        value = value + ref[base + LIFT : base + 2 * LIFT].astype(jnp.float32)
    return value


def put_split(refs, base, pieces, value):
    high = value.astype(jnp.bfloat16)
    low = (value - high.astype(jnp.float32)).astype(jnp.bfloat16)
    for ref in refs:
        ref[base : base + LIFT] = high
        if pieces == 2:
            ref[base + LIFT : base + 2 * LIFT] = low


def lifted_sum(ref, base, pieces):
    total = joined(ref.at[0], base, pieces)
    for k in range(1, RING):
        total = total + joined(ref.at[k], base, pieces)
    return total


def block_sum(ref, rows):
    total = ref[0, rows].astype(jnp.float32)
    for k in range(1, RING):
        total = total + ref[k, rows].astype(jnp.float32)
    return total


def join_kernel(lift, far_ref, out_ref):
    n = 2 * BLOCK
    for copy in range(RING):
        for k in range(RING):
            out_ref[copy, k * n : (k + 1) * n] = far_ref[k, :n]
    if lift:
        outs = [out_ref.at[copy] for copy in range(RING)]
        put_split(outs, RING * n, 2, lifted_sum(far_ref, n, 1))


def tile_kernel(lift, src_ref, dst_ref, weight_ref, own_ref, other_ref, near_ref, out_ref, acc_ref):
    acc_ref[...] = jnp.zeros_like(acc_ref)
    held = 2 * RING
    n = held * BLOCK
    slots = own_ref.shape[0]
    for half, tiles_ref in enumerate((own_ref, other_ref)):
        for t in range(slots):
            s = half * slots + t
            place = src_ref[s]
            row = pl.multiple_of(place % held * BLOCK, BLOCK)
            operand = near_ref[place // held, pl.ds(row, BLOCK)]
            term = jnp.dot(tiles_ref[t], operand, preferred_element_type=jnp.float32)
            acc_ref[dst_ref[s]] += weight_ref[s] * term
    for k in range(RING):
        sums = acc_ref[k * held : (k + 1) * held].astype(jnp.bfloat16)
        out_ref[k, :n] = sums.reshape(n, sums.shape[-1])
    if lift:
        outs = [out_ref.at[k] for k in range(RING)]
        put_split(outs, n, 2, lifted_sum(near_ref, n, 2))


def sum_kernel(lift, near_ref, out_ref):
    m = 2 * BLOCK
    for k in range(RING):
        out_ref[k, :m] = block_sum(near_ref, slice(k * m, (k + 1) * m)).astype(jnp.bfloat16)
    if lift:
        outs = [out_ref.at[k] for k in range(RING)]
        put_split(outs, m, 1, lifted_sum(near_ref, RING * m, 2))


def last_kernel(lift, far_ref, sums_ref, out_ref):
    m = 2 * BLOCK
    total = block_sum(far_ref, slice(0, m))
    sums_ref[...] = total
    if lift:
        out_ref[:BLOCK] = total[BLOCK:].astype(jnp.bfloat16)
        put_split([out_ref], BLOCK, 2, lifted_sum(far_ref, m, 1))
    else:
        out_ref[...] = total.astype(jnp.bfloat16)


def middle_kernel(
    core_ref, sums_ref, back_ref, both_ref, scale_ref, other_ref, weight_ref, bias_ref,
    cotangent_ref, activated_ref, out_ref,
):
    packed = other_ref[2 * BLOCK : 3 * BLOCK, :3].astype(jnp.float32)
    scales = (scale_ref[...], packed[:, 0:1] + packed[:, 1:2] + packed[:, 2:3])
    cotangents = (cotangent_ref[...], other_ref[BLOCK : 2 * BLOCK])
    grads = bias_grad = None
    for c in range(2):
        rows = slice(c * BLOCK, (c + 1) * BLOCK)
        back = back_ref[(1 - c) * BLOCK : (2 - c) * BLOCK].astype(jnp.float32)
        total = sums_ref[rows] + back + both_ref[0, rows].astype(jnp.float32)
        spread = total.astype(jnp.bfloat16)
        hidden = jnp.dot(spread, weight_ref[...], preferred_element_type=jnp.float32)
        preact = scales[c] * hidden + bias_ref[...]
        sig = jax.nn.sigmoid(preact)
        if c == 0:
            activated_ref[...] = (preact * sig).astype(jnp.bfloat16)
        delta = cotangents[c].astype(jnp.float32) * sig * (1.0 + preact * (1.0 - sig))
        scaled_delta = (scales[c] * delta).astype(jnp.bfloat16)
        for copy in range(RING):
            out_ref[copy, rows] = scaled_delta
        product = lax.dot_general(
            spread, scaled_delta, (((0,), (0,)), ((), ())), preferred_element_type=jnp.float32
        )
        column = jnp.sum(delta, axis=0, keepdims=True)
        grads = product if c == 0 else grads + product
        bias_grad = column if c == 0 else bias_grad + column
    pad = LIFT - HALF
    row = lax.broadcasted_iota(jnp.int32, (pad, grads.shape[1]), 0)
    top = jnp.concatenate([grads[:HALF], jnp.where(row == 0, bias_grad, 0.0)], axis=0)
    bottom = jnp.concatenate([grads[HALF:], jnp.zeros((pad, grads.shape[1]), jnp.float32)], axis=0)
    outs = [out_ref.at[copy] for copy in range(RING)]
    put_split(outs, 2 * BLOCK, 1, jnp.where(core_ref[0] == 0, top, bottom))


def end_kernel(
    core_ref, sums_ref, sent_ref, back_ref, both_ref, scale_ref, weight_ref,
    feature_grad_ref, weight_grad_ref, bias_grad_ref,
):
    total = sums_ref[:BLOCK] + back_ref[:BLOCK].astype(jnp.float32)
    total = total + both_ref[0, :BLOCK].astype(jnp.float32)
    proj_grad = (scale_ref[...] * total).astype(jnp.bfloat16)
    feature_grad_ref[...] = lax.dot_general(
        proj_grad, weight_ref[...], (((1,), (1,)), ((), ())), preferred_element_type=jnp.float32
    ).astype(jnp.bfloat16)
    first = core_ref[0] == 0
    here, there = joined(sent_ref, BLOCK, 2), joined(back_ref, BLOCK, 2)
    top = jnp.where(first, here, there)
    bottom = jnp.where(first, there, here)
    weight_grad_ref[:HALF] = top[:HALF]
    weight_grad_ref[HALF:] = bottom[:HALF]
    bias_grad_ref[...] = top[HALF : HALF + 1]


def shards(
    features, weight, bias, node_scale, cotangent, tile_row, tile_col, tile_count, tile_values
):
    row_pos = lax.axis_index("row")
    col_pos = lax.axis_index("col")
    core = row_pos % 2
    n_col = lax.axis_size("col")
    first = core == 0
    width = features.shape[1]

    rows_idx = tile_row[0, 0]
    cols_idx = tile_col[0, 0]
    tiles = tile_values[0, 0]
    slots = jnp.arange(rows_idx.shape[0], dtype=jnp.int32)
    same = row_pos * n_col + rows_idx == cols_idx * n_col + col_pos
    live = jnp.where(slots < tile_count[0, 0], jnp.where(same, 0.5, 1.0), 0.0)

    scale = node_scale[:, None]
    scaled = (scale * features.astype(jnp.float32)).astype(jnp.bfloat16)

    meta = jnp.stack([rows_idx.astype(jnp.float32), cols_idx.astype(jnp.float32), live])
    meta = jnp.pad(meta, ((0, 13), (0, 120))).astype(jnp.bfloat16)
    parts, packed = scale, []
    for _ in range(3):
        piece = lax.reduce_precision(parts, exponent_bits=8, mantissa_bits=7)
        packed.append(piece)
        parts = parts - piece
    packed = jnp.pad(jnp.concatenate(packed, axis=1), ((0, 0), (0, width - 3)))
    arrived = swap_cores(
        jnp.concatenate([scaled, cotangent, packed.astype(jnp.bfloat16), meta], axis=0)
    )
    tiles_other = swap_cores(tiles)
    own = jnp.where(first, tiles, jnp.swapaxes(tiles, 1, 2))
    other = jnp.where(first, tiles_other, jnp.swapaxes(tiles_other, 1, 2))
    meta_other = arrived[3 * BLOCK : 3 * BLOCK + 3, :8]
    rows_all = jnp.concatenate([rows_idx, meta_other[0].astype(jnp.int32)])
    cols_all = jnp.concatenate([cols_idx, meta_other[1].astype(jnp.int32)])
    weights = jnp.concatenate([live, meta_other[2].astype(jnp.float32)])
    foreign = jnp.concatenate([jnp.zeros_like(slots), jnp.ones_like(slots)])
    by_row = (cols_all // 2 % RING * RING + cols_all // (2 * RING)) * 2
    by_row = by_row + (cols_all % 2 != core).astype(jnp.int32)
    by_col = (rows_all // RING * RING + rows_all % RING) * 2 + foreign
    src = jnp.where(first, by_row, by_col)
    dst = jnp.where(first, by_col, by_row)
    bf16 = jnp.bfloat16

    def spread_sum(both, lift):
        n = 2 * RING * BLOCK + (2 * LIFT if lift else 0)
        (near,) = call(
            functools.partial(join_kernel, lift),
            [((RING, n, width), bf16)],
            exchange(both, 0, False),
        )
        (sums,) = call(
            functools.partial(tile_kernel, lift),
            [((RING, n, width), bf16)],
            src, dst, weights, own, other, exchange(near, 0, True),
            scalars=3,
            scratch=[pltpu.VMEM((2 * RING * RING, BLOCK, width), jnp.float32)],
        )
        (sums,) = call(
            functools.partial(sum_kernel, lift),
            [(both.shape, bf16)],
            exchange(sums, 1, True),
        )
        rows = BLOCK + 2 * LIFT if lift else 2 * BLOCK
        both_sums, sent = call(
            functools.partial(last_kernel, lift),
            [((2 * BLOCK, width), jnp.float32), ((rows, width), bf16)],
            exchange(sums, 1, False),
        )
        return both_sums, sent, swap_cores(sent)

    core_no = core.reshape(1)
    both = jnp.concatenate([scaled, arrived[:BLOCK]], axis=0)
    both = jnp.broadcast_to(both, (RING, 2 * BLOCK, width))

    sums, _, back = spread_sum(both, False)
    activated, both = call(
        middle_kernel,
        [((BLOCK, width), jnp.bfloat16), ((RING, 2 * BLOCK + LIFT, width), jnp.bfloat16)],
        core_no, sums, back, both, scale, arrived, weight, bias[None, :], cotangent,
        scalars=1,
    )
    sums, sent, back = spread_sum(both, True)
    feature_grad, weight_grad, bias_grad = call(
        end_kernel,
        [
            ((BLOCK, width), jnp.bfloat16),
            (weight.shape, jnp.float32),
            ((1, width), jnp.float32),
        ],
        core_no, sums, sent, back, both, scale, weight,
        scalars=1,
    )
    return activated, feature_grad, weight_grad, bias_grad[0]


def solution(mesh):
    placed = (
        P(AXES, None),
        P(),
        P(),
        P(AXES),
        P(AXES, None),
        P("row", "col", None),
        P("row", "col", None),
        P("row", "col"),
        P("row", "col", None, None, None),
    )
    return jax.shard_map(
        shards,
        mesh=mesh,
        in_specs=placed,
        out_specs=(P(AXES, None), P(AXES, None), P(), P()),
        check_vma=False,
    )
```

```python
import functools
import jax
import jax.numpy as jnp
from jax import lax
from jax.experimental import pallas as pl
from jax.experimental.pallas import tpu as pltpu
from jax.sharding import PartitionSpec as P

BLOCK = 256
RING = 4
HALF = 64
LIFT = 80
AXES = ("row", "col")


def rank(zl, x, core, y, zh):
    return ((zl * RING + x) * 2 + core) * RING * RING + y * RING + zh


def pairs(step):
    out = []
    for zl in range(RING):
        for x in range(RING):
            for core in range(2):
                for y in range(RING):
                    for zh in range(RING):
                        out.append((rank(zl, x, core, y, zh), rank(*step(zl, x, core, y, zh))))
    return out


def swap_cores(v):
    return lax.ppermute(v, AXES, pairs(lambda zl, x, core, y, zh: (zl, x, 1 - core, y, zh)))


def far_shift(v, k, row_core):
    def step(zl, x, core, y, zh):
        if core == row_core:
            return (zl + k) % RING, x, core, y, zh
        return zl, x, core, y, (zh + (k if zl % 2 == 0 else -k)) % RING

    return lax.ppermute(v, AXES, pairs(step))


def near_exchange(v, row_core):
    groups = []
    for core in range(2):
        for free in range(RING**3):
            i, j, k = free // RING**2, free // RING % RING, free % RING
            if core == row_core:
                groups.append([rank(i, m, core, j, k) for m in range(RING)])
            else:
                groups.append([rank(i, j, core, m, k) for m in range(RING)])
    return lax.all_to_all(
        v, AXES, split_axis=0, concat_axis=0, tiled=True, axis_index_groups=groups
    )


def call(kernel, outs, *operands, scalars=0, scratch=()):
    smem = pl.BlockSpec(memory_space=pltpu.SMEM)
    vmem = pl.BlockSpec(memory_space=pltpu.VMEM)
    return pl.pallas_call(
        kernel,
        out_shape=[jax.ShapeDtypeStruct(shape, dtype) for shape, dtype in outs],
        in_specs=[smem] * scalars + [vmem] * (len(operands) - scalars),
        out_specs=[vmem] * len(outs),
        scratch_shapes=list(scratch),
        compiler_params=pltpu.CompilerParams(vmem_limit_bytes=40 * 1024 * 1024),
    )(*operands)


def joined(ref, base, pieces):
    value = ref[base : base + LIFT].astype(jnp.float32)
    if pieces == 2:
        value = value + ref[base + LIFT : base + 2 * LIFT].astype(jnp.float32)
    return value


def put_split(refs, base, pieces, value):
    high = value.astype(jnp.bfloat16)
    low = (value - high.astype(jnp.float32)).astype(jnp.bfloat16)
    for ref in refs:
        ref[base : base + LIFT] = high
        if pieces == 2:
            ref[base + LIFT : base + 2 * LIFT] = low


def lifted_sum(parts, base, pieces):
    own, after, across, before = [joined(part, base, pieces) for part in parts]
    return (own + across) + (after + before)


def slots_of(ref):
    return [ref.at[k] for k in range(RING)]


def join_kernel(lift, *refs):
    parts, out_ref = refs[:RING], refs[RING]
    n = 2 * BLOCK
    for copy in range(RING):
        for k in range(RING):
            out_ref[copy, k * n : (k + 1) * n] = parts[k][:n]
    if lift:
        put_split(slots_of(out_ref), RING * n, 2, lifted_sum(parts, n, 1))


def tile_kernel(lift, src_ref, dst_ref, weight_ref, own_ref, other_ref, near_ref, out_ref, acc_ref):
    acc_ref[...] = jnp.zeros_like(acc_ref)
    held = 2 * RING
    n = held * BLOCK
    slots = own_ref.shape[0]
    for half, tiles_ref in enumerate((own_ref, other_ref)):
        for t in range(slots):
            s = half * slots + t
            place = src_ref[s]
            row = pl.multiple_of(place % held * BLOCK, BLOCK)
            operand = near_ref[place // held, pl.ds(row, BLOCK)]
            term = jnp.dot(tiles_ref[t], operand, preferred_element_type=jnp.float32)
            acc_ref[dst_ref[s]] += weight_ref[s] * term
    for k in range(RING):
        sums = acc_ref[k * held : (k + 1) * held].astype(jnp.bfloat16)
        out_ref[k, :n] = sums.reshape(n, sums.shape[-1])
    if lift:
        put_split(slots_of(out_ref), n, 2, lifted_sum(slots_of(near_ref), n, 2))


def sum_kernel(lift, near_ref, mine_ref, *outs):
    m = 2 * BLOCK
    for k in range(RING):
        rows = slice(k * m, (k + 1) * m)
        total = near_ref[0, rows].astype(jnp.float32)
        for j in range(1, RING):
            total = total + near_ref[j, rows].astype(jnp.float32)
        if k == 0:
            mine_ref[...] = total
        else:
            outs[k - 1][:m] = total.astype(jnp.bfloat16)
    if lift:
        put_split(outs, m, 1, lifted_sum(slots_of(near_ref), RING * m, 2))


def relay_kernel(lift, own_ref, passing_ref, out_ref):
    m = 2 * BLOCK
    total = own_ref[:m].astype(jnp.float32) + passing_ref[:m].astype(jnp.float32)
    out_ref[:m] = total.astype(jnp.bfloat16)
    if lift:
        out_ref[m:] = passing_ref[m:]


def last_kernel(lift, mine_ref, own_ref, after_ref, across_ref, before_ref, sums_ref, out_ref):
    m = 2 * BLOCK
    total = mine_ref[...]
    for part in (across_ref, before_ref):
        total = total + part[:m].astype(jnp.float32)
    sums_ref[...] = total
    if lift:
        out_ref[:BLOCK] = total[BLOCK:].astype(jnp.bfloat16)
        parts = (own_ref, after_ref, across_ref, before_ref)
        put_split([out_ref], BLOCK, 2, lifted_sum(parts, m, 1))
    else:
        out_ref[...] = total.astype(jnp.bfloat16)


def middle_kernel(
    core_ref, sums_ref, back_ref, both_ref, scale_ref, other_ref, weight_ref, bias_ref,
    cotangent_ref, activated_ref, out_ref,
):
    packed = other_ref[2 * BLOCK : 3 * BLOCK, :3].astype(jnp.float32)
    scales = (scale_ref[...], packed[:, 0:1] + packed[:, 1:2] + packed[:, 2:3])
    cotangents = (cotangent_ref[...], other_ref[BLOCK : 2 * BLOCK])
    grads = bias_grad = None
    for c in range(2):
        rows = slice(c * BLOCK, (c + 1) * BLOCK)
        back = back_ref[(1 - c) * BLOCK : (2 - c) * BLOCK].astype(jnp.float32)
        total = sums_ref[rows] + back + both_ref[rows].astype(jnp.float32)
        spread = total.astype(jnp.bfloat16)
        hidden = jnp.dot(spread, weight_ref[...], preferred_element_type=jnp.float32)
        preact = scales[c] * hidden + bias_ref[...]
        sig = jax.nn.sigmoid(preact)
        if c == 0:
            activated_ref[...] = (preact * sig).astype(jnp.bfloat16)
        delta = cotangents[c].astype(jnp.float32) * sig * (1.0 + preact * (1.0 - sig))
        scaled_delta = (scales[c] * delta).astype(jnp.bfloat16)
        out_ref[rows] = scaled_delta
        product = lax.dot_general(
            spread, scaled_delta, (((0,), (0,)), ((), ())), preferred_element_type=jnp.float32
        )
        column = jnp.sum(delta, axis=0, keepdims=True)
        grads = product if c == 0 else grads + product
        bias_grad = column if c == 0 else bias_grad + column
    pad = LIFT - HALF
    row = lax.broadcasted_iota(jnp.int32, (pad, grads.shape[1]), 0)
    top = jnp.concatenate([grads[:HALF], jnp.where(row == 0, bias_grad, 0.0)], axis=0)
    bottom = jnp.concatenate([grads[HALF:], jnp.zeros((pad, grads.shape[1]), jnp.float32)], axis=0)
    put_split([out_ref], 2 * BLOCK, 1, jnp.where(core_ref[0] == 0, top, bottom))


def end_kernel(
    core_ref, sums_ref, sent_ref, back_ref, both_ref, scale_ref, weight_ref,
    feature_grad_ref, weight_grad_ref, bias_grad_ref,
):
    total = sums_ref[:BLOCK] + back_ref[:BLOCK].astype(jnp.float32)
    total = total + both_ref[:BLOCK].astype(jnp.float32)
    proj_grad = (scale_ref[...] * total).astype(jnp.bfloat16)
    feature_grad_ref[...] = lax.dot_general(
        proj_grad, weight_ref[...], (((1,), (1,)), ((), ())), preferred_element_type=jnp.float32
    ).astype(jnp.bfloat16)
    first = core_ref[0] == 0
    here, there = joined(sent_ref, BLOCK, 2), joined(back_ref, BLOCK, 2)
    top = jnp.where(first, here, there)
    bottom = jnp.where(first, there, here)
    weight_grad_ref[:HALF] = top[:HALF]
    weight_grad_ref[HALF:] = bottom[:HALF]
    bias_grad_ref[...] = top[HALF : HALF + 1]


def shards(
    features, weight, bias, node_scale, cotangent, tile_row, tile_col, tile_count, tile_values
):
    row_pos = lax.axis_index("row")
    col_pos = lax.axis_index("col")
    core = row_pos % 2
    n_col = lax.axis_size("col")
    first = core == 0
    width = features.shape[1]

    rows_idx = tile_row[0, 0]
    cols_idx = tile_col[0, 0]
    tiles = tile_values[0, 0]
    slots = jnp.arange(rows_idx.shape[0], dtype=jnp.int32)
    same = row_pos * n_col + rows_idx == cols_idx * n_col + col_pos
    live = jnp.where(slots < tile_count[0, 0], jnp.where(same, 0.5, 1.0), 0.0)

    scale = node_scale[:, None]
    scaled = (scale * features.astype(jnp.float32)).astype(jnp.bfloat16)

    meta = jnp.stack([rows_idx.astype(jnp.float32), cols_idx.astype(jnp.float32), live])
    meta = jnp.pad(meta, ((0, 13), (0, 120))).astype(jnp.bfloat16)
    parts, packed = scale, []
    for _ in range(3):
        piece = lax.reduce_precision(parts, exponent_bits=8, mantissa_bits=7)
        packed.append(piece)
        parts = parts - piece
    packed = jnp.pad(jnp.concatenate(packed, axis=1), ((0, 0), (0, width - 3)))
    arrived = swap_cores(
        jnp.concatenate([scaled, cotangent, packed.astype(jnp.bfloat16), meta], axis=0)
    )
    tiles_other = swap_cores(tiles)
    own = jnp.where(first, tiles, jnp.swapaxes(tiles, 1, 2))
    other = jnp.where(first, tiles_other, jnp.swapaxes(tiles_other, 1, 2))
    meta_other = arrived[3 * BLOCK : 3 * BLOCK + 3, :8]
    rows_all = jnp.concatenate([rows_idx, meta_other[0].astype(jnp.int32)])
    cols_all = jnp.concatenate([cols_idx, meta_other[1].astype(jnp.int32)])
    weights = jnp.concatenate([live, meta_other[2].astype(jnp.float32)])
    foreign = jnp.concatenate([jnp.zeros_like(slots), jnp.ones_like(slots)])
    dzl = cols_all // (2 * RING) - row_pos // (2 * RING)
    dzh = (rows_all % RING - col_pos % RING) * (1 - 2 * (row_pos // (2 * RING) % 2))
    dcore = (cols_all % 2 != core).astype(jnp.int32)
    in_row = cols_all // 2 % RING * 2 * RING + dcore
    in_col = rows_all // RING * 2 * RING + foreign
    src = jnp.where(first, in_row + jnp.mod(-dzl, RING) * 2, in_col + jnp.mod(-dzh, RING) * 2)
    dst = jnp.where(first, in_col + jnp.mod(dzh, RING) * 2, in_row + jnp.mod(dzl, RING) * 2)
    bf16 = jnp.bfloat16

    def spread_sum(both, lift):
        n = 2 * RING * BLOCK + (2 * LIFT if lift else 0)
        after = far_shift(both, 1, 0)
        before = far_shift(both, -1, 0)
        across = far_shift(after, 1, 0)
        (near,) = call(
            functools.partial(join_kernel, lift),
            [((RING, n, width), bf16)],
            both, after, across, before,
        )
        (sums,) = call(
            functools.partial(tile_kernel, lift),
            [((RING, n, width), bf16)],
            src, dst, weights, own, other, near_exchange(near, 0),
            scalars=3,
            scratch=[pltpu.VMEM((2 * RING * RING, BLOCK, width), jnp.float32)],
        )
        mine, to_after, to_across, to_before = call(
            functools.partial(sum_kernel, lift),
            [((2 * BLOCK, width), jnp.float32)] + [(both.shape, bf16)] * 3,
            near_exchange(sums, 1),
        )
        after = far_shift(to_across, 1, 1)
        before = far_shift(to_before, -1, 1)
        (passed,) = call(
            functools.partial(relay_kernel, lift), [(both.shape, bf16)], to_after, after
        )
        across = far_shift(passed, 1, 1)
        rows = BLOCK + 2 * LIFT if lift else 2 * BLOCK
        both_sums, sent = call(
            functools.partial(last_kernel, lift),
            [((2 * BLOCK, width), jnp.float32), ((rows, width), bf16)],
            mine, to_after, after, across, before,
        )
        return both_sums, sent, swap_cores(sent)

    core_no = core.reshape(1)
    both = jnp.concatenate([scaled, arrived[:BLOCK]], axis=0)

    sums, _, back = spread_sum(both, False)
    activated, both = call(
        middle_kernel,
        [((BLOCK, width), jnp.bfloat16), ((2 * BLOCK + LIFT, width), jnp.bfloat16)],
        core_no, sums, back, both, scale, arrived, weight, bias[None, :], cotangent,
        scalars=1,
    )
    sums, sent, back = spread_sum(both, True)
    feature_grad, weight_grad, bias_grad = call(
        end_kernel,
        [
            ((BLOCK, width), jnp.bfloat16),
            (weight.shape, jnp.float32),
            ((1, width), jnp.float32),
        ],
        core_no, sums, sent, back, both, scale, weight,
        scalars=1,
    )
    return activated, feature_grad, weight_grad, bias_grad[0]


def solution(mesh):
    placed = (
        P(AXES, None),
        P(),
        P(),
        P(AXES),
        P(AXES, None),
        P("row", "col", None),
        P("row", "col", None),
        P("row", "col"),
        P("row", "col", None, None, None),
    )
    return jax.shard_map(
        shards,
        mesh=mesh,
        in_specs=placed,
        out_specs=(P(AXES, None), P(AXES, None), P(), P()),
        check_vma=False,
    )
```

```python
import functools
import jax
import jax.numpy as jnp
from jax import lax
from jax.experimental import pallas as pl
from jax.experimental.pallas import tpu as pltpu
from jax.sharding import PartitionSpec as P

BLOCK = 256
RING = 4
HALF = 64
LIFT = 80
AXES = ("row", "col")


def rank(zl, x, core, y, zh):
    return ((zl * RING + x) * 2 + core) * RING * RING + y * RING + zh


def pairs(step):
    out = []
    for zl in range(RING):
        for x in range(RING):
            for core in range(2):
                for y in range(RING):
                    for zh in range(RING):
                        out.append((rank(zl, x, core, y, zh), rank(*step(zl, x, core, y, zh))))
    return out


def swap_cores(v):
    return lax.ppermute(v, AXES, pairs(lambda zl, x, core, y, zh: (zl, x, 1 - core, y, zh)))


def far_shift(v, k, row_core):
    def step(zl, x, core, y, zh):
        if core == row_core:
            return (zl + k) % RING, x, core, y, zh
        return zl, x, core, y, (zh + (k if zl % 2 == 0 else -k)) % RING

    return lax.ppermute(v, AXES, pairs(step))


def near_exchange(v, row_core):
    groups = []
    for core in range(2):
        for free in range(RING**3):
            i, j, k = free // RING**2, free // RING % RING, free % RING
            if core == row_core:
                groups.append([rank(i, m, core, j, k) for m in range(RING)])
            else:
                groups.append([rank(i, j, core, m, k) for m in range(RING)])
    return lax.all_to_all(
        v, AXES, split_axis=0, concat_axis=0, tiled=True, axis_index_groups=groups
    )


def call(kernel, outs, *operands, scalars=0, scratch=(), mebibytes=8, in_place=False):
    smem = pl.BlockSpec(memory_space=pltpu.SMEM)
    vmem = pl.BlockSpec(memory_space=pl.ANY if in_place else pltpu.VMEM)
    return pl.pallas_call(
        kernel,
        out_shape=[jax.ShapeDtypeStruct(shape, dtype) for shape, dtype in outs],
        in_specs=[smem] * scalars + [vmem] * (len(operands) - scalars),
        out_specs=[pl.BlockSpec(memory_space=pltpu.VMEM)] * len(outs),
        scratch_shapes=list(scratch),
        compiler_params=pltpu.CompilerParams(vmem_limit_bytes=mebibytes * 1024 * 1024),
    )(*operands)


def joined(ref, base, pieces):
    value = ref[base : base + LIFT].astype(jnp.float32)
    if pieces == 2:
        value = value + ref[base + LIFT : base + 2 * LIFT].astype(jnp.float32)
    return value


def put_split(refs, base, pieces, value):
    high = value.astype(jnp.bfloat16)
    low = (value - high.astype(jnp.float32)).astype(jnp.bfloat16)
    for ref in refs:
        ref[base : base + LIFT] = high
        if pieces == 2:
            ref[base + LIFT : base + 2 * LIFT] = low


def lifted_sum(parts, base, pieces):
    own, after, across, before = [joined(part, base, pieces) for part in parts]
    return (own + across) + (after + before)


def slots_of(ref):
    return [ref.at[k] for k in range(RING)]


def pack_kernel(*refs):
    sources, out_ref, landed, sems = refs[:7], refs[7], refs[8:-1], refs[-1]
    tiles_ref = sources[-1]
    landed = landed + (out_ref.at[pl.ds(2 * BLOCK, tiles_ref.shape[0])],)
    copies = [
        pltpu.make_async_copy(source, target, sems.at[k])
        for k, (source, target) in enumerate(zip(sources, landed))
    ]
    for copy in copies:
        copy.start()
    row_ref, col_ref, count_ref, features_ref, cotangent_ref, scale_ref = landed[:-1]
    for copy in copies[:-1]:
        copy.wait()
    lines, width = scale_ref.shape
    out_ref[:BLOCK, width:] = cotangent_ref[...]
    lane = lax.broadcasted_iota(jnp.int32, (width, width), 1)
    line = lax.broadcasted_iota(jnp.int32, (width, width), 0)
    for half in range(lines):
        row = scale_ref[half : half + 1]
        scale = jnp.sum(jnp.where(lane == line, row, 0.0), axis=1, keepdims=True)
        rows = slice(half * width, (half + 1) * width)
        scaled = scale * features_ref[rows].astype(jnp.float32)
        out_ref[rows, :width] = scaled.astype(jnp.bfloat16)
        packed = jnp.zeros((width, width), jnp.float32)
        rest = scale
        for k in range(3):
            piece = rest.astype(jnp.bfloat16).astype(jnp.float32)
            packed = jnp.where(lane == k, piece, packed)
            rest = rest - piece
        start = BLOCK + half * width
        out_ref[start : start + width, :width] = packed.astype(jnp.bfloat16)
    row_pos, col_pos = lax.axis_index("row"), lax.axis_index("col")
    n_col = lax.axis_size("col")
    shape = (16, width)
    lane = lax.broadcasted_iota(jnp.int32, shape, 1)
    line = lax.broadcasted_iota(jnp.int32, shape, 0)
    meta = jnp.zeros(shape, jnp.float32)
    for t in range(row_ref.shape[2]):
        i, j = row_ref[0, 0, t], col_ref[0, 0, t]
        same = row_pos * n_col + i == j * n_col + col_pos
        live = jnp.where(t < count_ref[0, 0], jnp.where(same, 0.5, 1.0), 0.0)
        for k, value in enumerate((i.astype(jnp.float32), j.astype(jnp.float32), live)):
            meta = jnp.where((line == k) & (lane == t), value, meta)
    out_ref[BLOCK : BLOCK + 16, width:] = meta.astype(jnp.bfloat16)
    out_ref[BLOCK + 16 : 2 * BLOCK, width:] = jnp.zeros((BLOCK - 16, width), jnp.bfloat16)
    copies[-1].wait()


def scale_of(facts_ref):
    packed = facts_ref[BLOCK : 2 * BLOCK, :3].astype(jnp.float32)
    return packed[:, 0:1] + packed[:, 1:2] + packed[:, 2:3]


def join_kernel(lift, *refs):
    parts, out_ref = refs[:RING], refs[RING]
    n = 2 * BLOCK
    for copy in range(RING):
        for k in range(RING):
            out_ref[copy, k * n : (k + 1) * n] = parts[k][:n]
    if lift:
        put_split(slots_of(out_ref), RING * n, 2, lifted_sum(parts, n, 1))


def tile_kernel(
    lift, core_ref, src_ref, dst_ref, weight_ref, own_ref, other_ref, near_ref, out_ref, acc_ref
):
    acc_ref[...] = jnp.zeros_like(acc_ref)
    held = 2 * RING
    n = held * BLOCK
    slots = (own_ref.shape[0] - 2 * BLOCK) // BLOCK

    def products(contracted):
        for half, tiles_ref in enumerate((own_ref, other_ref)):
            for t in range(slots):
                s = half * slots + t
                place = src_ref[s]
                row = pl.multiple_of(place % held * BLOCK, BLOCK)
                term = lax.dot_general(
                    tiles_ref[(t + 2) * BLOCK : (t + 3) * BLOCK],
                    near_ref[place // held, pl.ds(row, BLOCK)],
                    (((contracted,), (0,)), ((), ())),
                    preferred_element_type=jnp.float32,
                )
                acc_ref[dst_ref[s]] += weight_ref[s] * term

    @pl.when(core_ref[0] == 0)
    def _():
        products(1)

    @pl.when(core_ref[0] != 0)
    def _():
        products(0)

    for k in range(RING):
        sums = acc_ref[k * held : (k + 1) * held].astype(jnp.bfloat16)
        out_ref[k, :n] = sums.reshape(n, sums.shape[-1])
    if lift:
        put_split(slots_of(out_ref), n, 2, lifted_sum(slots_of(near_ref), n, 2))


def sum_kernel(lift, near_ref, mine_ref, *outs):
    m = 2 * BLOCK
    for k in range(RING):
        rows = slice(k * m, (k + 1) * m)
        total = near_ref[0, rows].astype(jnp.float32)
        for j in range(1, RING):
            total = total + near_ref[j, rows].astype(jnp.float32)
        if k == 0:
            mine_ref[...] = total
        else:
            outs[k - 1][:m] = total.astype(jnp.bfloat16)
    if lift:
        put_split(outs, m, 1, lifted_sum(slots_of(near_ref), RING * m, 2))


def relay_kernel(lift, own_ref, passing_ref, out_ref):
    m = 2 * BLOCK
    total = own_ref[:m].astype(jnp.float32) + passing_ref[:m].astype(jnp.float32)
    out_ref[:m] = total.astype(jnp.bfloat16)
    if lift:
        out_ref[m:] = passing_ref[m:]


def last_kernel(lift, mine_ref, own_ref, after_ref, across_ref, before_ref, sums_ref, out_ref):
    m = 2 * BLOCK
    total = mine_ref[...]
    for part in (across_ref, before_ref):
        total = total + part[:m].astype(jnp.float32)
    sums_ref[...] = total
    if lift:
        out_ref[:BLOCK] = total[BLOCK:].astype(jnp.bfloat16)
        parts = (own_ref, after_ref, across_ref, before_ref)
        put_split([out_ref], BLOCK, 2, lifted_sum(parts, m, 1))
    else:
        out_ref[...] = total.astype(jnp.bfloat16)


def middle_kernel(
    core_ref, sums_ref, back_ref, both_ref, facts_ref, other_ref, weight_ref, bias_ref,
    activated_ref, out_ref,
):
    scales = (scale_of(facts_ref), scale_of(other_ref))
    width = out_ref.shape[1]
    cotangents = (facts_ref[:BLOCK, width:], other_ref[:BLOCK, width:])
    grads = bias_grad = None
    for c in range(2):
        rows = slice(c * BLOCK, (c + 1) * BLOCK)
        back = back_ref[(1 - c) * BLOCK : (2 - c) * BLOCK].astype(jnp.float32)
        total = sums_ref[rows] + back + both_ref[rows].astype(jnp.float32)
        spread = total.astype(jnp.bfloat16)
        hidden = jnp.dot(spread, weight_ref[...], preferred_element_type=jnp.float32)
        preact = scales[c] * hidden + bias_ref[...]
        sig = jax.nn.sigmoid(preact)
        if c == 0:
            activated_ref[...] = (preact * sig).astype(jnp.bfloat16)
        delta = cotangents[c].astype(jnp.float32) * sig * (1.0 + preact * (1.0 - sig))
        scaled_delta = (scales[c] * delta).astype(jnp.bfloat16)
        out_ref[rows] = scaled_delta
        product = lax.dot_general(
            spread, scaled_delta, (((0,), (0,)), ((), ())), preferred_element_type=jnp.float32
        )
        column = jnp.sum(delta, axis=0, keepdims=True)
        grads = product if c == 0 else grads + product
        bias_grad = column if c == 0 else bias_grad + column
    pad = LIFT - HALF
    row = lax.broadcasted_iota(jnp.int32, (pad, grads.shape[1]), 0)
    top = jnp.concatenate([grads[:HALF], jnp.where(row == 0, bias_grad, 0.0)], axis=0)
    bottom = jnp.concatenate([grads[HALF:], jnp.zeros((pad, grads.shape[1]), jnp.float32)], axis=0)
    put_split([out_ref], 2 * BLOCK, 1, jnp.where(core_ref[0] == 0, top, bottom))


def end_kernel(
    core_ref, sums_ref, sent_ref, back_ref, both_ref, facts_ref, weight_ref,
    feature_grad_ref, weight_grad_ref, bias_grad_ref,
):
    total = sums_ref[:BLOCK] + back_ref[:BLOCK].astype(jnp.float32)
    total = total + both_ref[:BLOCK].astype(jnp.float32)
    proj_grad = (scale_of(facts_ref) * total).astype(jnp.bfloat16)
    feature_grad_ref[...] = lax.dot_general(
        proj_grad, weight_ref[...], (((1,), (1,)), ((), ())), preferred_element_type=jnp.float32
    ).astype(jnp.bfloat16)
    first = core_ref[0] == 0
    here, there = joined(sent_ref, BLOCK, 2), joined(back_ref, BLOCK, 2)
    top = jnp.where(first, here, there)
    bottom = jnp.where(first, there, here)
    weight_grad_ref[:HALF] = top[:HALF]
    weight_grad_ref[HALF:] = bottom[:HALF]
    bias_grad_ref[...] = top[HALF : HALF + 1]


def shards(
    features, weight, bias, node_scale, cotangent, tile_row, tile_col, tile_count, tile_values
):
    row_pos = lax.axis_index("row")
    col_pos = lax.axis_index("col")
    core = row_pos % 2
    n_col = lax.axis_size("col")
    core_no = core.reshape(1)
    first = core == 0
    width = features.shape[1]

    rows_idx = tile_row[0, 0]
    cols_idx = tile_col[0, 0]
    tiles = tile_values[0, 0]
    slots = jnp.arange(rows_idx.shape[0], dtype=jnp.int32)
    same = row_pos * n_col + rows_idx == cols_idx * n_col + col_pos
    live = jnp.where(slots < tile_count[0, 0], jnp.where(same, 0.5, 1.0), 0.0)

    (facts,) = call(
        pack_kernel,
        [((2 * BLOCK + tiles.shape[0] * BLOCK, BLOCK), jnp.bfloat16)],
        tile_row, tile_col, tile_count, features, cotangent, node_scale.reshape(2, -1),
        tiles.reshape(-1, BLOCK),
        scratch=[
            pltpu.SMEM(tile_row.shape, jnp.int32),
            pltpu.SMEM(tile_col.shape, jnp.int32),
            pltpu.SMEM(tile_count.shape, jnp.int32),
            pltpu.VMEM(features.shape, jnp.bfloat16),
            pltpu.VMEM(cotangent.shape, jnp.bfloat16),
            pltpu.VMEM((2, width), jnp.float32),
            pltpu.SemaphoreType.DMA((7,)),
        ],
        mebibytes=60,
        in_place=True,
    )
    arrived = swap_cores(facts)
    meta_other = arrived[BLOCK : BLOCK + 3, width : width + tiles.shape[0]]

    rows_all = jnp.concatenate([rows_idx, meta_other[0].astype(jnp.int32)])
    cols_all = jnp.concatenate([cols_idx, meta_other[1].astype(jnp.int32)])
    weights = jnp.concatenate([live, meta_other[2].astype(jnp.float32)])
    foreign = jnp.concatenate([jnp.zeros_like(slots), jnp.ones_like(slots)])
    dzl = cols_all // (2 * RING) - row_pos // (2 * RING)
    dzh = (rows_all % RING - col_pos % RING) * (1 - 2 * (row_pos // (2 * RING) % 2))
    dcore = (cols_all % 2 != core).astype(jnp.int32)
    in_row = cols_all // 2 % RING * 2 * RING + dcore
    in_col = rows_all // RING * 2 * RING + foreign
    src = jnp.where(first, in_row + jnp.mod(-dzl, RING) * 2, in_col + jnp.mod(-dzh, RING) * 2)
    dst = jnp.where(first, in_col + jnp.mod(dzh, RING) * 2, in_row + jnp.mod(dzl, RING) * 2)
    bf16 = jnp.bfloat16

    def spread_sum(both, lift):
        n = 2 * RING * BLOCK + (2 * LIFT if lift else 0)
        after = far_shift(both, 1, 0)
        before = far_shift(both, -1, 0)
        across = far_shift(after, 1, 0)
        (near,) = call(
            functools.partial(join_kernel, lift),
            [((RING, n, width), bf16)],
            both, after, across, before,
        )
        (sums,) = call(
            functools.partial(tile_kernel, lift),
            [((RING, n, width), bf16)],
            core_no, src, dst, weights, facts, arrived, near_exchange(near, 0),
            scalars=4,
            scratch=[pltpu.VMEM((2 * RING * RING, BLOCK, width), jnp.float32)],
            mebibytes=20,
        )
        mine, to_after, to_across, to_before = call(
            functools.partial(sum_kernel, lift),
            [((2 * BLOCK, width), jnp.float32)] + [(both.shape, bf16)] * 3,
            near_exchange(sums, 1),
        )
        after = far_shift(to_across, 1, 1)
        before = far_shift(to_before, -1, 1)
        (passed,) = call(
            functools.partial(relay_kernel, lift), [(both.shape, bf16)], to_after, after
        )
        across = far_shift(passed, 1, 1)
        rows = BLOCK + 2 * LIFT if lift else 2 * BLOCK
        both_sums, sent = call(
            functools.partial(last_kernel, lift),
            [((2 * BLOCK, width), jnp.float32), ((rows, width), bf16)],
            mine, to_after, after, across, before,
        )
        return both_sums, sent, swap_cores(sent)

    both = jnp.concatenate([facts[:BLOCK, :width], arrived[:BLOCK, :width]], axis=0)

    sums, _, back = spread_sum(both, False)
    activated, both = call(
        middle_kernel,
        [((BLOCK, width), jnp.bfloat16), ((2 * BLOCK + LIFT, width), jnp.bfloat16)],
        core_no, sums, back, both, facts, arrived, weight, bias[None, :],
        scalars=1,
    )
    sums, sent, back = spread_sum(both, True)
    feature_grad, weight_grad, bias_grad = call(
        end_kernel,
        [
            ((BLOCK, width), jnp.bfloat16),
            (weight.shape, jnp.float32),
            ((1, width), jnp.float32),
        ],
        core_no, sums, sent, back, both, facts, weight,
        scalars=1,
    )
    return activated, feature_grad, weight_grad, bias_grad[0]


def solution(mesh):
    placed = (
        P(AXES, None),
        P(),
        P(),
        P(AXES),
        P(AXES, None),
        P("row", "col", None),
        P("row", "col", None),
        P("row", "col"),
        P("row", "col", None, None, None),
    )
    return jax.shard_map(
        shards,
        mesh=mesh,
        in_specs=placed,
        out_specs=(P(AXES, None), P(AXES, None), P(), P()),
        check_vma=False,
    )
```

```python
import functools
import jax
import jax.numpy as jnp
from jax import lax
from jax.experimental import pallas as pl
from jax.experimental.pallas import tpu as pltpu
from jax.sharding import PartitionSpec as P

BLOCK = 256
RING = 4
HALF = 64
LIFT = 80
AXES = ("row", "col")


def rank(zl, x, core, y, zh):
    return ((zl * RING + x) * 2 + core) * RING * RING + y * RING + zh


def pairs(step):
    out = []
    for zl in range(RING):
        for x in range(RING):
            for core in range(2):
                for y in range(RING):
                    for zh in range(RING):
                        out.append((rank(zl, x, core, y, zh), rank(*step(zl, x, core, y, zh))))
    return out


def swap_cores(v):
    return lax.ppermute(v, AXES, pairs(lambda zl, x, core, y, zh: (zl, x, 1 - core, y, zh)))


def far_shift(v, k, row_core):
    def step(zl, x, core, y, zh):
        if core == row_core:
            return (zl + k) % RING, x, core, y, zh
        return zl, x, core, y, (zh + (k if zl % 2 == 0 else -k)) % RING

    return lax.ppermute(v, AXES, pairs(step))


def near_exchange(v, row_core):
    groups = []
    for core in range(2):
        for free in range(RING**3):
            i, j, k = free // RING**2, free // RING % RING, free % RING
            if core == row_core:
                groups.append([rank(i, m, core, j, k) for m in range(RING)])
            else:
                groups.append([rank(i, j, core, m, k) for m in range(RING)])
    return lax.all_to_all(
        v, AXES, split_axis=0, concat_axis=0, tiled=True, axis_index_groups=groups
    )


def call(kernel, outs, *operands, scalars=0, scratch=(), mebibytes=8, in_place=False):
    smem = pl.BlockSpec(memory_space=pltpu.SMEM)
    vmem = pl.BlockSpec(memory_space=pl.ANY if in_place else pltpu.VMEM)
    return pl.pallas_call(
        kernel,
        out_shape=[jax.ShapeDtypeStruct(shape, dtype) for shape, dtype in outs],
        in_specs=[smem] * scalars + [vmem] * (len(operands) - scalars),
        out_specs=[pl.BlockSpec(memory_space=pltpu.VMEM)] * len(outs),
        scratch_shapes=list(scratch),
        compiler_params=pltpu.CompilerParams(vmem_limit_bytes=mebibytes * 1024 * 1024),
    )(*operands)


def joined(ref, base, pieces):
    value = ref[base : base + LIFT].astype(jnp.float32)
    if pieces == 2:
        value = value + ref[base + LIFT : base + 2 * LIFT].astype(jnp.float32)
    return value


def put_split(refs, base, pieces, value):
    high = value.astype(jnp.bfloat16)
    low = (value - high.astype(jnp.float32)).astype(jnp.bfloat16)
    for ref in refs:
        ref[base : base + LIFT] = high
        if pieces == 2:
            ref[base + LIFT : base + 2 * LIFT] = low


def lifted_sum(parts, base, pieces):
    own, after, across, before = [joined(part, base, pieces) for part in parts]
    return (own + across) + (after + before)


def slots_of(ref):
    return [ref.at[k] for k in range(RING)]


def pack_kernel(*refs):
    sources, out_ref, landed, sems = refs[:7], refs[7], refs[8:-1], refs[-1]
    tiles_ref = sources[-1]
    landed = landed + (out_ref.at[pl.ds(2 * BLOCK, tiles_ref.shape[0])],)
    copies = [
        pltpu.make_async_copy(source, target, sems.at[k])
        for k, (source, target) in enumerate(zip(sources, landed))
    ]
    for copy in copies:
        copy.start()
    row_ref, col_ref, count_ref, features_ref, cotangent_ref, scale_ref = landed[:-1]
    for copy in copies[:-1]:
        copy.wait()
    lines, width = scale_ref.shape
    out_ref[:BLOCK, width:] = cotangent_ref[...]
    lane = lax.broadcasted_iota(jnp.int32, (width, width), 1)
    line = lax.broadcasted_iota(jnp.int32, (width, width), 0)
    for half in range(lines):
        row = scale_ref[half : half + 1]
        scale = jnp.sum(jnp.where(lane == line, row, 0.0), axis=1, keepdims=True)
        rows = slice(half * width, (half + 1) * width)
        scaled = scale * features_ref[rows].astype(jnp.float32)
        out_ref[rows, :width] = scaled.astype(jnp.bfloat16)
        packed = jnp.zeros((width, width), jnp.float32)
        rest = scale
        for k in range(3):
            piece = rest.astype(jnp.bfloat16).astype(jnp.float32)
            packed = jnp.where(lane == k, piece, packed)
            rest = rest - piece
        start = BLOCK + half * width
        out_ref[start : start + width, :width] = packed.astype(jnp.bfloat16)
    row_pos, col_pos = lax.axis_index("row"), lax.axis_index("col")
    n_col = lax.axis_size("col")
    shape = (16, width)
    lane = lax.broadcasted_iota(jnp.int32, shape, 1)
    line = lax.broadcasted_iota(jnp.int32, shape, 0)
    meta = jnp.zeros(shape, jnp.float32)
    for t in range(row_ref.shape[2]):
        i, j = row_ref[0, 0, t], col_ref[0, 0, t]
        same = row_pos * n_col + i == j * n_col + col_pos
        live = jnp.where(t < count_ref[0, 0], jnp.where(same, 0.5, 1.0), 0.0)
        for k, value in enumerate((i.astype(jnp.float32), j.astype(jnp.float32), live)):
            meta = jnp.where((line == k) & (lane == t), value, meta)
    out_ref[BLOCK : BLOCK + 16, width:] = meta.astype(jnp.bfloat16)
    out_ref[BLOCK + 16 : 2 * BLOCK, width:] = jnp.zeros((BLOCK - 16, width), jnp.bfloat16)
    copies[-1].wait()


def scale_of(facts_ref):
    packed = facts_ref[BLOCK : 2 * BLOCK, :3].astype(jnp.float32)
    return packed[:, 0:1] + packed[:, 1:2] + packed[:, 2:3]


def join_kernel(lift, *refs):
    parts, out_ref = refs[:RING], refs[RING]
    n = 2 * BLOCK
    for copy in range(RING):
        for k in range(RING):
            out_ref[copy, k * n : (k + 1) * n] = parts[k][:n]
    if lift:
        put_split(slots_of(out_ref), RING * n, 2, lifted_sum(parts, n, 1))


def tile_kernel(
    lift, core_ref, src_ref, dst_ref, weight_ref, own_ref, other_ref, near_ref, out_ref, acc_ref
):
    acc_ref[...] = jnp.zeros_like(acc_ref)
    held = 2 * RING
    n = held * BLOCK
    slots = (own_ref.shape[0] - 2 * BLOCK) // BLOCK

    def products(contracted):
        for half, tiles_ref in enumerate((own_ref, other_ref)):
            for t in range(slots):
                s = half * slots + t
                place = src_ref[s]
                row = pl.multiple_of(place % held * BLOCK, BLOCK)
                term = lax.dot_general(
                    tiles_ref[(t + 2) * BLOCK : (t + 3) * BLOCK],
                    near_ref[place // held, pl.ds(row, BLOCK)],
                    (((contracted,), (0,)), ((), ())),
                    preferred_element_type=jnp.float32,
                )
                acc_ref[dst_ref[s]] += weight_ref[s] * term

    @pl.when(core_ref[0] == 0)
    def _():
        products(1)

    @pl.when(core_ref[0] != 0)
    def _():
        products(0)

    for k in range(RING):
        sums = acc_ref[k * held : (k + 1) * held].astype(jnp.bfloat16)
        out_ref[k, :n] = sums.reshape(n, sums.shape[-1])
    if lift:
        put_split(slots_of(out_ref), n, 2, lifted_sum(slots_of(near_ref), n, 2))


def sum_kernel(lift, near_ref, mine_ref, *outs):
    m = 2 * BLOCK
    for k in range(RING):
        rows = slice(k * m, (k + 1) * m)
        total = near_ref[0, rows].astype(jnp.float32)
        for j in range(1, RING):
            total = total + near_ref[j, rows].astype(jnp.float32)
        if k == 0:
            mine_ref[...] = total
        else:
            outs[k - 1][:m] = total.astype(jnp.bfloat16)
    if lift:
        put_split(outs, m, 1, lifted_sum(slots_of(near_ref), RING * m, 2))


def relay_kernel(lift, own_ref, passing_ref, out_ref):
    m = 2 * BLOCK
    total = own_ref[:m].astype(jnp.float32) + passing_ref[:m].astype(jnp.float32)
    out_ref[:m] = total.astype(jnp.bfloat16)
    if lift:
        out_ref[m:] = passing_ref[m:]


def last_kernel(lift, mine_ref, own_ref, after_ref, across_ref, before_ref, sums_ref, out_ref):
    m = 2 * BLOCK
    total = mine_ref[...]
    for part in (across_ref, before_ref):
        total = total + part[:m].astype(jnp.float32)
    sums_ref[...] = total
    if lift:
        out_ref[:BLOCK] = total[BLOCK:].astype(jnp.bfloat16)
        parts = (own_ref, after_ref, across_ref, before_ref)
        put_split([out_ref], BLOCK, 2, lifted_sum(parts, m, 1))
    else:
        out_ref[...] = total.astype(jnp.bfloat16)


def middle_kernel(
    core_ref, sums_ref, back_ref, both_ref, facts_ref, other_ref, weight_ref, bias_ref,
    activated_ref, out_ref,
):
    scales = (scale_of(facts_ref), scale_of(other_ref))
    width = out_ref.shape[1]
    cotangents = (facts_ref[:BLOCK, width:], other_ref[:BLOCK, width:])
    grads = bias_grad = None
    for c in range(2):
        rows = slice(c * BLOCK, (c + 1) * BLOCK)
        back = back_ref[(1 - c) * BLOCK : (2 - c) * BLOCK].astype(jnp.float32)
        total = sums_ref[rows] + back + both_ref[rows].astype(jnp.float32)
        spread = total.astype(jnp.bfloat16)
        hidden = jnp.dot(spread, weight_ref[...], preferred_element_type=jnp.float32)
        preact = scales[c] * hidden + bias_ref[...]
        sig = jax.nn.sigmoid(preact)
        if c == 0:
            activated_ref[...] = (preact * sig).astype(jnp.bfloat16)
        delta = cotangents[c].astype(jnp.float32) * sig * (1.0 + preact * (1.0 - sig))
        scaled_delta = (scales[c] * delta).astype(jnp.bfloat16)
        out_ref[rows] = scaled_delta
        product = lax.dot_general(
            spread, scaled_delta, (((0,), (0,)), ((), ())), preferred_element_type=jnp.float32
        )
        column = jnp.sum(delta, axis=0, keepdims=True)
        grads = product if c == 0 else grads + product
        bias_grad = column if c == 0 else bias_grad + column
    pad = LIFT - HALF
    row = lax.broadcasted_iota(jnp.int32, (pad, grads.shape[1]), 0)
    top = jnp.concatenate([grads[:HALF], jnp.where(row == 0, bias_grad, 0.0)], axis=0)
    bottom = jnp.concatenate([grads[HALF:], jnp.zeros((pad, grads.shape[1]), jnp.float32)], axis=0)
    put_split([out_ref], 2 * BLOCK, 1, jnp.where(core_ref[0] == 0, top, bottom))


def end_kernel(
    core_ref, sums_ref, sent_ref, back_ref, both_ref, facts_ref, weight_ref,
    feature_grad_ref, weight_grad_ref, bias_grad_ref,
):
    total = sums_ref[:BLOCK] + back_ref[:BLOCK].astype(jnp.float32)
    total = total + both_ref[:BLOCK].astype(jnp.float32)
    proj_grad = (scale_of(facts_ref) * total).astype(jnp.bfloat16)
    feature_grad_ref[...] = lax.dot_general(
        proj_grad, weight_ref[...], (((1,), (1,)), ((), ())), preferred_element_type=jnp.float32
    ).astype(jnp.bfloat16)
    first = core_ref[0] == 0
    here, there = joined(sent_ref, BLOCK, 2), joined(back_ref, BLOCK, 2)
    top = jnp.where(first, here, there)
    bottom = jnp.where(first, there, here)
    weight_grad_ref[:HALF] = top[:HALF]
    weight_grad_ref[HALF:] = bottom[:HALF]
    bias_grad_ref[...] = top[HALF : HALF + 1]


def shards(
    features, weight, bias, node_scale, cotangent, tile_row, tile_col, tile_count, tile_values
):
    row_pos = lax.axis_index("row")
    col_pos = lax.axis_index("col")
    core = row_pos % 2
    n_col = lax.axis_size("col")
    core_no = core.reshape(1)
    first = core == 0
    width = features.shape[1]

    rows_idx = tile_row[0, 0]
    cols_idx = tile_col[0, 0]
    tiles = tile_values[0, 0]
    slots = jnp.arange(rows_idx.shape[0], dtype=jnp.int32)
    same = row_pos * n_col + rows_idx == cols_idx * n_col + col_pos
    live = jnp.where(slots < tile_count[0, 0], jnp.where(same, 0.5, 1.0), 0.0)

    (facts,) = call(
        pack_kernel,
        [((2 * BLOCK + tiles.shape[0] * BLOCK, BLOCK), jnp.bfloat16)],
        tile_row, tile_col, tile_count, features, cotangent, node_scale.reshape(2, -1),
        tiles.reshape(-1, BLOCK),
        scratch=[
            pltpu.SMEM(tile_row.shape, jnp.int32),
            pltpu.SMEM(tile_col.shape, jnp.int32),
            pltpu.SMEM(tile_count.shape, jnp.int32),
            pltpu.VMEM(features.shape, jnp.bfloat16),
            pltpu.VMEM(cotangent.shape, jnp.bfloat16),
            pltpu.VMEM((2, width), jnp.float32),
            pltpu.SemaphoreType.DMA((7,)),
        ],
        mebibytes=60,
        in_place=True,
    )
    arrived = swap_cores(facts)
    meta_other = arrived[BLOCK : BLOCK + 3, width : width + tiles.shape[0]]

    rows_all = jnp.concatenate([rows_idx, meta_other[0].astype(jnp.int32)])
    cols_all = jnp.concatenate([cols_idx, meta_other[1].astype(jnp.int32)])
    weights = jnp.concatenate([live, meta_other[2].astype(jnp.float32)])
    foreign = jnp.concatenate([jnp.zeros_like(slots), jnp.ones_like(slots)])
    dzl = cols_all // (2 * RING) - row_pos // (2 * RING)
    dzh = (rows_all % RING - col_pos % RING) * (1 - 2 * (row_pos // (2 * RING) % 2))
    dcore = (cols_all % 2 != core).astype(jnp.int32)
    in_row = cols_all // 2 % RING * 2 * RING + dcore
    in_col = rows_all // RING * 2 * RING + foreign
    src = jnp.where(first, in_row + jnp.mod(-dzl, RING) * 2, in_col + jnp.mod(-dzh, RING) * 2)
    dst = jnp.where(first, in_col + jnp.mod(dzh, RING) * 2, in_row + jnp.mod(dzl, RING) * 2)
    bf16 = jnp.bfloat16
    places = (src, dst, weights)

    def spread_sum(both, places, lift):
        n = 2 * RING * BLOCK + (2 * LIFT if lift else 0)
        after = far_shift(both, 1, 0)
        held, places = lax.optimization_barrier((both, places))
        before = far_shift(held, -1, 0)
        across = far_shift(after, 1, 0)
        (near,) = call(
            functools.partial(join_kernel, lift),
            [((RING, n, width), bf16)],
            both, after, across, before,
        )
        near, places = lax.optimization_barrier((near, places))
        (sums,) = call(
            functools.partial(tile_kernel, lift),
            [((RING, n, width), bf16)],
            core_no, *places, facts, arrived, near_exchange(near, 0),
            scalars=4,
            scratch=[pltpu.VMEM((2 * RING * RING, BLOCK, width), jnp.float32)],
            mebibytes=20,
        )
        mine, to_after, to_across, to_before = call(
            functools.partial(sum_kernel, lift),
            [((2 * BLOCK, width), jnp.float32)] + [(both.shape, bf16)] * 3,
            near_exchange(sums, 1),
        )
        after = far_shift(to_across, 1, 1)
        before = far_shift(to_before, -1, 1)
        (passed,) = call(
            functools.partial(relay_kernel, lift), [(both.shape, bf16)], to_after, after
        )
        across = far_shift(passed, 1, 1)
        rows = BLOCK + 2 * LIFT if lift else 2 * BLOCK
        both_sums, sent = call(
            functools.partial(last_kernel, lift),
            [((2 * BLOCK, width), jnp.float32), ((rows, width), bf16)],
            mine, to_after, after, across, before,
        )
        return both_sums, sent, swap_cores(sent)

    both = jnp.concatenate([facts[:BLOCK, :width], arrived[:BLOCK, :width]], axis=0)

    sums, _, back = spread_sum(both, places, False)
    activated, both = call(
        middle_kernel,
        [((BLOCK, width), jnp.bfloat16), ((2 * BLOCK + LIFT, width), jnp.bfloat16)],
        core_no, sums, back, both, facts, arrived, weight, bias[None, :],
        scalars=1,
    )
    sums, sent, back = spread_sum(both, places, True)
    feature_grad, weight_grad, bias_grad = call(
        end_kernel,
        [
            ((BLOCK, width), jnp.bfloat16),
            (weight.shape, jnp.float32),
            ((1, width), jnp.float32),
        ],
        core_no, sums, sent, back, both, facts, weight,
        scalars=1,
    )
    return activated, feature_grad, weight_grad, bias_grad[0]


def solution(mesh):
    placed = (
        P(AXES, None),
        P(),
        P(),
        P(AXES),
        P(AXES, None),
        P("row", "col", None),
        P("row", "col", None),
        P("row", "col"),
        P("row", "col", None, None, None),
    )
    return jax.shard_map(
        shards,
        mesh=mesh,
        in_specs=placed,
        out_specs=(P(AXES, None), P(AXES, None), P(), P()),
        check_vma=False,
    )
```

```python
import functools
import jax
import jax.numpy as jnp
from jax import lax
from jax.experimental import pallas as pl
from jax.experimental.pallas import tpu as pltpu
from jax.sharding import PartitionSpec as P

BLOCK = 256
RING = 4
HALF = 64
LIFT = 80
AXES = ("row", "col")


def rank(zl, x, core, y, zh):
    return ((zl * RING + x) * 2 + core) * RING * RING + y * RING + zh


def pairs(step):
    out = []
    for zl in range(RING):
        for x in range(RING):
            for core in range(2):
                for y in range(RING):
                    for zh in range(RING):
                        out.append((rank(zl, x, core, y, zh), rank(*step(zl, x, core, y, zh))))
    return out


def swap_cores(v):
    return lax.ppermute(v, AXES, pairs(lambda zl, x, core, y, zh: (zl, x, 1 - core, y, zh)))


def far_shift(v, k, row_core):
    def step(zl, x, core, y, zh):
        if core == row_core:
            return (zl + k) % RING, x, core, y, zh
        return zl, x, core, y, (zh + (k if zl % 2 == 0 else -k)) % RING

    return lax.ppermute(v, AXES, pairs(step))


def near_exchange(v, row_core):
    groups = []
    for core in range(2):
        for free in range(RING**3):
            i, j, k = free // RING**2, free // RING % RING, free % RING
            if core == row_core:
                groups.append([rank(i, m, core, j, k) for m in range(RING)])
            else:
                groups.append([rank(i, j, core, m, k) for m in range(RING)])
    return lax.all_to_all(
        v, AXES, split_axis=0, concat_axis=0, tiled=True, axis_index_groups=groups
    )


def call(kernel, outs, *operands, scalars=0, scratch=(), mebibytes=8, in_place=False):
    smem = pl.BlockSpec(memory_space=pltpu.SMEM)
    vmem = pl.BlockSpec(memory_space=pl.ANY if in_place else pltpu.VMEM)
    return pl.pallas_call(
        kernel,
        out_shape=[jax.ShapeDtypeStruct(shape, dtype) for shape, dtype in outs],
        in_specs=[smem] * scalars + [vmem] * (len(operands) - scalars),
        out_specs=[pl.BlockSpec(memory_space=pltpu.VMEM)] * len(outs),
        scratch_shapes=list(scratch),
        compiler_params=pltpu.CompilerParams(vmem_limit_bytes=mebibytes * 1024 * 1024),
    )(*operands)


def joined(ref, base, pieces):
    value = ref[base : base + LIFT].astype(jnp.float32)
    if pieces == 2:
        value = value + ref[base + LIFT : base + 2 * LIFT].astype(jnp.float32)
    return value


def put_split(refs, base, pieces, value):
    high = value.astype(jnp.bfloat16)
    low = (value - high.astype(jnp.float32)).astype(jnp.bfloat16)
    for ref in refs:
        ref[base : base + LIFT] = high
        if pieces == 2:
            ref[base + LIFT : base + 2 * LIFT] = low


def lifted_sum(parts, base, pieces):
    own, after, across, before = [joined(part, base, pieces) for part in parts]
    return (own + across) + (after + before)


def slots_of(ref):
    return [ref.at[k] for k in range(RING)]


def pack_kernel(*refs):
    sources, out_ref, landed, sems = refs[:7], refs[7], refs[8:-1], refs[-1]
    tiles_ref = sources[-1]
    landed = landed + (out_ref.at[pl.ds(2 * BLOCK, tiles_ref.shape[0])],)
    copies = [
        pltpu.make_async_copy(source, target, sems.at[k])
        for k, (source, target) in enumerate(zip(sources, landed))
    ]
    for copy in copies:
        copy.start()
    row_ref, col_ref, count_ref, features_ref, cotangent_ref, scale_ref = landed[:-1]
    for copy in copies[:-1]:
        copy.wait()
    lines, width = scale_ref.shape
    out_ref[:BLOCK, width:] = cotangent_ref[...]
    lane = lax.broadcasted_iota(jnp.int32, (width, width), 1)
    line = lax.broadcasted_iota(jnp.int32, (width, width), 0)
    for half in range(lines):
        row = scale_ref[half : half + 1]
        scale = jnp.sum(jnp.where(lane == line, row, 0.0), axis=1, keepdims=True)
        rows = slice(half * width, (half + 1) * width)
        scaled = scale * features_ref[rows].astype(jnp.float32)
        out_ref[rows, :width] = scaled.astype(jnp.bfloat16)
        packed = jnp.zeros((width, width), jnp.float32)
        rest = scale
        for k in range(3):
            piece = rest.astype(jnp.bfloat16).astype(jnp.float32)
            packed = jnp.where(lane == k, piece, packed)
            rest = rest - piece
        start = BLOCK + half * width
        out_ref[start : start + width, :width] = packed.astype(jnp.bfloat16)
    row_pos, col_pos = lax.axis_index("row"), lax.axis_index("col")
    n_col = lax.axis_size("col")
    shape = (16, width)
    lane = lax.broadcasted_iota(jnp.int32, shape, 1)
    line = lax.broadcasted_iota(jnp.int32, shape, 0)
    meta = jnp.zeros(shape, jnp.float32)
    for t in range(row_ref.shape[2]):
        i, j = row_ref[0, 0, t], col_ref[0, 0, t]
        same = row_pos * n_col + i == j * n_col + col_pos
        live = jnp.where(t < count_ref[0, 0], jnp.where(same, 0.5, 1.0), 0.0)
        for k, value in enumerate((i.astype(jnp.float32), j.astype(jnp.float32), live)):
            meta = jnp.where((line == k) & (lane == t), value, meta)
    out_ref[BLOCK : BLOCK + 16, width:] = meta.astype(jnp.bfloat16)
    out_ref[BLOCK + 16 : 2 * BLOCK, width:] = jnp.zeros((BLOCK - 16, width), jnp.bfloat16)
    copies[-1].wait()


def scale_of(facts_ref):
    packed = facts_ref[BLOCK : 2 * BLOCK, :3].astype(jnp.float32)
    return packed[:, 0:1] + packed[:, 1:2] + packed[:, 2:3]


def join_kernel(lift, *refs):
    parts, out_ref = refs[:RING], refs[RING]
    n = 2 * BLOCK
    for copy in range(RING):
        for k in range(RING):
            out_ref[copy, k * n : (k + 1) * n] = parts[k][:n]
    if lift:
        put_split(slots_of(out_ref), RING * n, 1, lifted_sum(parts, n, 1))


def tile_kernel(
    lift, core_ref, src_ref, dst_ref, weight_ref, own_ref, other_ref, near_ref, out_ref, acc_ref
):
    acc_ref[...] = jnp.zeros_like(acc_ref)
    held = 2 * RING
    n = held * BLOCK
    slots = (own_ref.shape[0] - 2 * BLOCK) // BLOCK

    def products(contracted):
        for half, tiles_ref in enumerate((own_ref, other_ref)):
            for t in range(slots):
                s = half * slots + t
                place = src_ref[s]
                row = pl.multiple_of(place % held * BLOCK, BLOCK)
                term = lax.dot_general(
                    tiles_ref[(t + 2) * BLOCK : (t + 3) * BLOCK],
                    near_ref[place // held, pl.ds(row, BLOCK)],
                    (((contracted,), (0,)), ((), ())),
                    preferred_element_type=jnp.float32,
                )
                acc_ref[dst_ref[s]] += weight_ref[s] * term

    @pl.when(core_ref[0] == 0)
    def _():
        products(1)

    @pl.when(core_ref[0] != 0)
    def _():
        products(0)

    for k in range(RING):
        sums = acc_ref[k * held : (k + 1) * held].astype(jnp.bfloat16)
        out_ref[k, :n] = sums.reshape(n, sums.shape[-1])
    if lift:
        put_split(slots_of(out_ref), n, 1, lifted_sum(slots_of(near_ref), n, 1))


def sum_kernel(lift, near_ref, mine_ref, *outs):
    m = 2 * BLOCK
    for k in range(RING):
        rows = slice(k * m, (k + 1) * m)
        total = near_ref[0, rows].astype(jnp.float32)
        for j in range(1, RING):
            total = total + near_ref[j, rows].astype(jnp.float32)
        if k == 0:
            mine_ref[...] = total
        else:
            outs[k - 1][:m] = total.astype(jnp.bfloat16)
    if lift:
        put_split(outs, m, 1, lifted_sum(slots_of(near_ref), RING * m, 1))


def relay_kernel(lift, own_ref, passing_ref, out_ref):
    m = 2 * BLOCK
    total = own_ref[:m].astype(jnp.float32) + passing_ref[:m].astype(jnp.float32)
    out_ref[:m] = total.astype(jnp.bfloat16)
    if lift:
        out_ref[m:] = passing_ref[m:]


def last_kernel(lift, mine_ref, own_ref, after_ref, across_ref, before_ref, sums_ref, out_ref):
    m = 2 * BLOCK
    total = mine_ref[...]
    for part in (across_ref, before_ref):
        total = total + part[:m].astype(jnp.float32)
    sums_ref[...] = total
    if lift:
        out_ref[:BLOCK] = total[BLOCK:].astype(jnp.bfloat16)
        parts = (own_ref, after_ref, across_ref, before_ref)
        put_split([out_ref], BLOCK, 2, lifted_sum(parts, m, 1))
    else:
        out_ref[...] = total.astype(jnp.bfloat16)


def middle_kernel(
    core_ref, sums_ref, back_ref, both_ref, facts_ref, other_ref, weight_ref, bias_ref,
    activated_ref, out_ref,
):
    scales = (scale_of(facts_ref), scale_of(other_ref))
    width = out_ref.shape[1]
    cotangents = (facts_ref[:BLOCK, width:], other_ref[:BLOCK, width:])
    grads = bias_grad = None
    for c in range(2):
        rows = slice(c * BLOCK, (c + 1) * BLOCK)
        back = back_ref[(1 - c) * BLOCK : (2 - c) * BLOCK].astype(jnp.float32)
        total = sums_ref[rows] + back + both_ref[rows].astype(jnp.float32)
        spread = total.astype(jnp.bfloat16)
        hidden = jnp.dot(spread, weight_ref[...], preferred_element_type=jnp.float32)
        preact = scales[c] * hidden + bias_ref[...]
        sig = jax.nn.sigmoid(preact)
        if c == 0:
            activated_ref[...] = (preact * sig).astype(jnp.bfloat16)
        delta = cotangents[c].astype(jnp.float32) * sig * (1.0 + preact * (1.0 - sig))
        scaled_delta = (scales[c] * delta).astype(jnp.bfloat16)
        out_ref[rows] = scaled_delta
        product = lax.dot_general(
            spread, scaled_delta, (((0,), (0,)), ((), ())), preferred_element_type=jnp.float32
        )
        column = jnp.sum(delta, axis=0, keepdims=True)
        grads = product if c == 0 else grads + product
        bias_grad = column if c == 0 else bias_grad + column
    pad = LIFT - HALF
    row = lax.broadcasted_iota(jnp.int32, (pad, grads.shape[1]), 0)
    top = jnp.concatenate([grads[:HALF], jnp.where(row == 0, bias_grad, 0.0)], axis=0)
    bottom = jnp.concatenate([grads[HALF:], jnp.zeros((pad, grads.shape[1]), jnp.float32)], axis=0)
    put_split([out_ref], 2 * BLOCK, 1, jnp.where(core_ref[0] == 0, top, bottom))


def end_kernel(
    core_ref, sums_ref, sent_ref, back_ref, both_ref, facts_ref, weight_ref,
    feature_grad_ref, weight_grad_ref, bias_grad_ref,
):
    total = sums_ref[:BLOCK] + back_ref[:BLOCK].astype(jnp.float32)
    total = total + both_ref[:BLOCK].astype(jnp.float32)
    proj_grad = (scale_of(facts_ref) * total).astype(jnp.bfloat16)
    feature_grad_ref[...] = lax.dot_general(
        proj_grad, weight_ref[...], (((1,), (1,)), ((), ())), preferred_element_type=jnp.float32
    ).astype(jnp.bfloat16)
    first = core_ref[0] == 0
    here, there = joined(sent_ref, BLOCK, 2), joined(back_ref, BLOCK, 2)
    top = jnp.where(first, here, there)
    bottom = jnp.where(first, there, here)
    weight_grad_ref[:HALF] = top[:HALF]
    weight_grad_ref[HALF:] = bottom[:HALF]
    bias_grad_ref[...] = top[HALF : HALF + 1]


def shards(
    features, weight, bias, node_scale, cotangent, tile_row, tile_col, tile_count, tile_values
):
    row_pos = lax.axis_index("row")
    col_pos = lax.axis_index("col")
    core = row_pos % 2
    n_col = lax.axis_size("col")
    core_no = core.reshape(1)
    first = core == 0
    width = features.shape[1]

    rows_idx = tile_row[0, 0]
    cols_idx = tile_col[0, 0]
    tiles = tile_values[0, 0]
    slots = jnp.arange(rows_idx.shape[0], dtype=jnp.int32)
    same = row_pos * n_col + rows_idx == cols_idx * n_col + col_pos
    live = jnp.where(slots < tile_count[0, 0], jnp.where(same, 0.5, 1.0), 0.0)

    (facts,) = call(
        pack_kernel,
        [((2 * BLOCK + tiles.shape[0] * BLOCK, BLOCK), jnp.bfloat16)],
        tile_row, tile_col, tile_count, features, cotangent, node_scale.reshape(2, -1),
        tiles.reshape(-1, BLOCK),
        scratch=[
            pltpu.SMEM(tile_row.shape, jnp.int32),
            pltpu.SMEM(tile_col.shape, jnp.int32),
            pltpu.SMEM(tile_count.shape, jnp.int32),
            pltpu.VMEM(features.shape, jnp.bfloat16),
            pltpu.VMEM(cotangent.shape, jnp.bfloat16),
            pltpu.VMEM((2, width), jnp.float32),
            pltpu.SemaphoreType.DMA((7,)),
        ],
        mebibytes=60,
        in_place=True,
    )
    arrived = swap_cores(facts)
    meta_other = arrived[BLOCK : BLOCK + 3, width : width + tiles.shape[0]]

    rows_all = jnp.concatenate([rows_idx, meta_other[0].astype(jnp.int32)])
    cols_all = jnp.concatenate([cols_idx, meta_other[1].astype(jnp.int32)])
    weights = jnp.concatenate([live, meta_other[2].astype(jnp.float32)])
    foreign = jnp.concatenate([jnp.zeros_like(slots), jnp.ones_like(slots)])
    dzl = cols_all // (2 * RING) - row_pos // (2 * RING)
    dzh = (rows_all % RING - col_pos % RING) * (1 - 2 * (row_pos // (2 * RING) % 2))
    dcore = (cols_all % 2 != core).astype(jnp.int32)
    in_row = cols_all // 2 % RING * 2 * RING + dcore
    in_col = rows_all // RING * 2 * RING + foreign
    src = jnp.where(first, in_row + jnp.mod(-dzl, RING) * 2, in_col + jnp.mod(-dzh, RING) * 2)
    dst = jnp.where(first, in_col + jnp.mod(dzh, RING) * 2, in_row + jnp.mod(dzl, RING) * 2)
    bf16 = jnp.bfloat16
    places = (src, dst, weights)

    def spread_sum(both, places, lift):
        n = 2 * RING * BLOCK + (LIFT if lift else 0)
        after = far_shift(both, 1, 0)
        held, places = lax.optimization_barrier((both, places))
        before = far_shift(held, -1, 0)
        across = far_shift(after, 1, 0)
        (near,) = call(
            functools.partial(join_kernel, lift),
            [((RING, n, width), bf16)],
            both, after, across, before,
        )
        near, places = lax.optimization_barrier((near, places))
        (sums,) = call(
            functools.partial(tile_kernel, lift),
            [((RING, n, width), bf16)],
            core_no, *places, facts, arrived, near_exchange(near, 0),
            scalars=4,
            scratch=[pltpu.VMEM((2 * RING * RING, BLOCK, width), jnp.float32)],
            mebibytes=20,
        )
        mine, to_after, to_across, to_before = call(
            functools.partial(sum_kernel, lift),
            [((2 * BLOCK, width), jnp.float32)] + [(both.shape, bf16)] * 3,
            near_exchange(sums, 1),
        )
        after = far_shift(to_across, 1, 1)
        before = far_shift(to_before, -1, 1)
        (passed,) = call(
            functools.partial(relay_kernel, lift), [(both.shape, bf16)], to_after, after
        )
        across = far_shift(passed, 1, 1)
        rows = BLOCK + 2 * LIFT if lift else 2 * BLOCK
        both_sums, sent = call(
            functools.partial(last_kernel, lift),
            [((2 * BLOCK, width), jnp.float32), ((rows, width), bf16)],
            mine, to_after, after, across, before,
        )
        return both_sums, sent, swap_cores(sent)

    both = jnp.concatenate([facts[:BLOCK, :width], arrived[:BLOCK, :width]], axis=0)

    sums, _, back = spread_sum(both, places, False)
    activated, both = call(
        middle_kernel,
        [((BLOCK, width), jnp.bfloat16), ((2 * BLOCK + LIFT, width), jnp.bfloat16)],
        core_no, sums, back, both, facts, arrived, weight, bias[None, :],
        scalars=1,
    )
    sums, sent, back = spread_sum(both, places, True)
    feature_grad, weight_grad, bias_grad = call(
        end_kernel,
        [
            ((BLOCK, width), jnp.bfloat16),
            (weight.shape, jnp.float32),
            ((1, width), jnp.float32),
        ],
        core_no, sums, sent, back, both, facts, weight,
        scalars=1,
    )
    return activated, feature_grad, weight_grad, bias_grad[0]


def solution(mesh):
    placed = (
        P(AXES, None),
        P(),
        P(),
        P(AXES),
        P(AXES, None),
        P("row", "col", None),
        P("row", "col", None),
        P("row", "col"),
        P("row", "col", None, None, None),
    )
    return jax.shard_map(
        shards,
        mesh=mesh,
        in_specs=placed,
        out_specs=(P(AXES, None), P(AXES, None), P(), P()),
        check_vma=False,
    )
```
